256 devices in a mesh: tm: 64 (over z, x, core), tensor: 4 (over y).
Axes of the slice: x: 4, y: 4, z: 8, core: 2. Of those that a mesh axis runs over, the one named last changes fastest.
Arguments:
- enc_frames: bfloat16 [96000, 1280], P('tm'), may hold values from -1.5 to 1.5
- span_counts: int32 [8], replicated, may hold values from 1 to 16, 64 in all
- enc_gain: float32 [1280], replicated, may hold values from 0.1 to 1.9
- enc_wq: bfloat16 [1280, 1024], P(None, 'tensor'), as said below
- enc_wk: bfloat16 [1280, 1024], P(None, 'tensor'), as said below
- enc_wv: bfloat16 [1280, 1024], P(None, 'tensor'), may hold values from -0.15625 to 0.15625
- enc_wo: bfloat16 [1024, 1280], P('tensor'), may hold values from -0.1875 to 0.1875
- adapter: bfloat16 [1280, 3584], P(None, 'tensor'), may hold values from -0.15625 to 0.15625
- owner_map: int32 [24000, 1], replicated, may hold values from 0 to 63; in each aligned block of 375 rows (0 to 374, 375 to 749, ...) at most 7 rows name the same one
- text_embeds: bfloat16 [4096, 3584], P('tm'), may hold values from -6 to 6
- llm_gain: float32 [3584], replicated, may hold values from 0.1 to 1.9
- llm_wq: bfloat16 [3584, 3584], P('tm', 'tensor'), as said below
- llm_wk: bfloat16 [3584, 512], P('tm', 'tensor'), as said below
- llm_wv: bfloat16 [3584, 512], P('tm', 'tensor'), may hold values from -0.09375 to 0.09375
- llm_bq: float32 [3584], P('tensor'), may hold values from -3 to 3
- llm_bk: float32 [512], P('tensor'), may hold values from -3 to 3
- llm_bv: float32 [512], P('tensor'), may hold values from -3 to 3
Outputs:
- context: bfloat16 [32768, 3584], P('tm', 'tensor')
The draws below stay inside these ranges and needn't reach their ends.
Inputs may be any that keep to these rules, and one draw needn't show every extreme that they name: `owner_map`: in each aligned block of 375 rows (the pooled frames of one device along tm), no owner is named by more than 7 rows. `span_counts`: the counts sum to 64. `enc_wq`: A projection matrix scaled by the inverse square root of its fan-in. `enc_wk`: A projection matrix scaled by the inverse square root of its fan-in. `llm_wq`: A projection matrix scaled by the inverse square root of its fan-in. `llm_wk`: A projection matrix scaled by the inverse square root of its fan-in.
All inputs are finite; a program needn't handle non-finite values.
Results may differ from the reference program's by a relative error of at most 0.03.
Values may be sent and summed in bfloat16 or wider, within the bound.
A program may use at most 128 MiB of HBM per device.

```python
import math
import jax
import jax.numpy as jnp
import numpy as np
from jax import lax

D_ENC = 1280
ENC_HEADS = 16
ENC_HD = 64
FRAMES = 1500
POOL = 4
CH_DEV = 1
D_LLM = 3584
Q_HEADS = 28
KV_HEADS = 4
LLM_HD = 128
SLOTS = 448
TEXT = 64
POOLED = 375
SPANS = 64
RECS = 8
SEND_CAP = 7
ROWS = 512
N_TM = 64
N_TENSOR = 4


def drawn_base(key, salt, rows, cols):
    return jax.random.normal(jax.random.fold_in(key, salt), (rows, cols), jnp.float32)


def draw_enc_wk(key, part):
    shared_base = drawn_base(key, 977, D_ENC, ENC_HEADS * ENC_HD)
    return (shared_base * D_ENC ** (-0.5)).astype(jnp.bfloat16)


def draw_enc_wq(key, part):
    key = jax.random.fold_in(key, 12)
    noise_part = jax.random.normal(key, (D_ENC, ENC_HEADS * ENC_HD), jnp.float32)
    mixed = noise_part
    return (mixed * D_ENC ** (-0.5)).astype(jnp.bfloat16)


def draw_llm_wk(key, part):
    shared_base = drawn_base(key, 978, D_LLM, KV_HEADS * LLM_HD)
    return (shared_base * D_LLM ** (-0.5)).astype(jnp.bfloat16)


def draw_llm_wq(key, part):
    key = jax.random.fold_in(key, 22)
    noise_part = jax.random.normal(key, (D_LLM, Q_HEADS * LLM_HD), jnp.float32)
    mixed = noise_part
    return (mixed * D_LLM ** (-0.5)).astype(jnp.bfloat16)


def shard_levels(stream_key, dims, cuts, smallest, top_value):
    factor_of = 1.0
    for position, parts in cuts:
        heights = jax.random.uniform(jax.random.fold_in(jax.random.fold_in(stream_key, 6), position), (parts,), jnp.float32, smallest / len(cuts), top_value / len(cuts))
        factor_of = factor_of * jnp.repeat(jnp.exp(heights), dims[position] // parts).reshape((-1,) + (1,) * (len(dims) - 1 - position))
    return factor_of


def length_profile(number_of, total, limit, skew):
    loads = [(1 << 20) // math.isqrt(grade ** skew) + 1 for grade in range(2, number_of + 1)]
    surplus, counts = total - limit - (number_of - 1), [1] * (number_of - 1)
    while surplus > 0:
        candidates = [i for i in range(number_of - 1) if counts[i] < limit]
        mass, budget = sum([loads[i] for i in candidates]), surplus
        for i in candidates:
            more = min(limit - counts[i], max(1, budget * loads[i] // mass), surplus)
            counts[i] = counts[i] + more
            surplus = surplus - more
    return np.array([limit] + counts)


def ragged(key, count, total, bound, skew):
    if count == 2:
        one = jax.random.randint(key, (), max(1, total - bound), min(bound, total - 1) + 1)
        return jnp.stack([one, total - one])
    lengths = jnp.asarray(length_profile(count, total, bound, skew), jnp.int32)
    twos = (count - 1) // 2
    giver, taker = lengths[1:1 + 2 * twos:2], lengths[2:2 + 2 * twos:2]
    room = jnp.minimum(giver - 1, bound - taker)
    shifted = jax.random.randint(jax.random.fold_in(key, 1), (twos,), 0, 1 << 20) % (room + 1)
    lengths = lengths.at[1:1 + 2 * twos:2].set(giver - shifted).at[2:2 + 2 * twos:2].set(taker + shifted)
    return lengths[jax.random.permutation(jax.random.fold_in(key, 2), count)]


def shared_out(own_key, own, number, rows, number_of, top, bound, slope):
    order = jax.random.permutation(own_key, number_of)
    heavy_load, common = shares(number_of, rows * top, bound, slope, True), shares(number_of, rows * top, bound, slope, False)
    places = jnp.arange(number_of)

    def named(sizes, turn):
        used = int((sizes > 0).sum())
        fixed = max(1, used // 4)
        passed = fixed + (places - fixed + turn * (used - fixed)) % max(1, number_of - fixed)
        return jnp.zeros((number_of,), jnp.int32).at[order[jnp.where(places < fixed, places, passed)]].set(jnp.asarray(sizes, jnp.int32))

    sizes = jnp.where(number % 4 == 0, named(heavy_load, number // 4), named(common, number - number // 4 - 1))
    mixed = jax.random.permutation(jax.random.fold_in(own, 3), number_of)
    donor, taker = mixed[0:number_of // 2 * 2:2], mixed[1:number_of // 2 * 2:2]
    margin = jnp.minimum(sizes[donor] - 1, bound - sizes[taker]) // 2
    margin = jnp.where((donor == order[0]) | (taker == order[0]) | (sizes[taker] == 0), 0, jnp.maximum(margin, 0))
    passed = jax.random.randint(jax.random.fold_in(own, 4), (number_of // 2,), 0, 1 << 20) % (margin + 1)
    sizes = sizes.at[donor].add(-passed).at[taker].add(passed)
    labels = jnp.searchsorted(jnp.cumsum(sizes), jnp.arange(rows * top), side="right").astype(jnp.int32)
    listing = labels.reshape(top, rows).T
    listing = listing[jax.random.permutation(jax.random.fold_in(own, 1), rows)]
    turn = jax.random.randint(jax.random.fold_in(own, 2), (rows, 1), 0, top)
    return jnp.take_along_axis(listing, (jnp.arange(top)[None, :] + turn) % top, axis=1)


def shares(count, total, limit, skew, full):
    weights = [(1 << 20) // math.isqrt(grade ** skew) + 1 for grade in range(1, count + 1)]
    largest = limit if full else min(limit, max(-(-total // count), total * weights[0] // sum(weights)))
    least = 1 if total - largest >= count - 1 else 0
    counts, rest = [largest] + [least] * (count - 1), total - largest - least * (count - 1)
    while rest > 0:
        free = [i for i in range(1, count) if counts[i] < largest] or [i for i in range(1, count) if counts[i] < limit]
        mass, budget = sum([weights[i] for i in free]), rest
        for i in free:
            more = min(limit - counts[i], max(1, budget * weights[i] // mass), rest)
            counts[i] = counts[i] + more
            rest = rest - more
    return np.array(counts)


def bell_draw(key, shape, deviation, most, split=(), held_as=jnp.bfloat16):
    factor_of = shard_levels(key, shape, split, -0.22, 0.18) if split else 1.0
    array = jax.random.normal(key, shape, jnp.float32) * deviation * factor_of
    return jnp.minimum(jnp.maximum(array, -most), most).astype(held_as)


def setup_inputs(seed: int = 0) -> dict:
    streams_of = jax.random.split(jax.random.key(seed), 18)
    enc_frames = bell_draw(streams_of[0], (SPANS * FRAMES, D_ENC), 0.25, 1.5, ((0, 64),))
    span_counts = ragged(streams_of[1], RECS, SPANS, min(16, SPANS), 2).astype(jnp.int32)
    enc_gain = jnp.clip(1.0 + 0.18 * jax.random.normal(streams_of[2], (D_ENC,), jnp.float32), 0.1, 1.9)
    enc_wq = draw_enc_wq(jax.random.fold_in(streams_of[17], 71), 0)
    enc_wk = draw_enc_wk(jax.random.fold_in(streams_of[17], 71), 0)
    enc_wv = bell_draw(streams_of[5], (D_ENC, ENC_HEADS * ENC_HD), D_ENC ** -0.5, 0.15625, ((1, 4),))
    enc_wo = bell_draw(streams_of[6], (ENC_HEADS * ENC_HD, D_ENC), (ENC_HEADS * ENC_HD) ** -0.5, 0.1875, ((0, 4),))
    adapter = bell_draw(streams_of[7], (D_ENC, D_LLM), D_ENC ** -0.5, 0.15625, ((1, 4),))
    owner_map_keys = jax.random.split(jax.random.fold_in(streams_of[8], 1), (SPANS * POOLED) // (CH_DEV * POOLED))
    owner_map_turns = jax.random.permutation(jax.random.fold_in(streams_of[8], 3), (SPANS * POOLED) // (CH_DEV * POOLED))
    owner_map = jax.vmap(lambda own, number: shared_out(jax.random.fold_in(streams_of[8], 2), own, number, CH_DEV * POOLED, N_TM, 1, SLOTS // N_TM, 2))(owner_map_keys, owner_map_turns).reshape((SPANS * POOLED, 1))
    text_embeds = bell_draw(streams_of[9], (N_TM * TEXT, D_LLM), 1.0, 6.0, ((0, 64),))
    llm_gain = jnp.clip(1.0 + 0.18 * jax.random.normal(streams_of[10], (D_LLM,), jnp.float32), 0.1, 1.9)
    llm_wq = draw_llm_wq(jax.random.fold_in(streams_of[17], 71), 0)
    llm_wk = draw_llm_wk(jax.random.fold_in(streams_of[17], 71), 0)
    llm_wv = bell_draw(streams_of[13], (D_LLM, KV_HEADS * LLM_HD), D_LLM ** -0.5, 0.09375, ((0, 64), (1, 4)))
    llm_bq = bell_draw(streams_of[14], (Q_HEADS * LLM_HD,), 0.5, 3.0, ((0, 4),), jnp.float32)
    llm_bk = bell_draw(streams_of[15], (KV_HEADS * LLM_HD,), 0.5, 3.0, ((0, 4),), jnp.float32)
    llm_bv = bell_draw(streams_of[16], (KV_HEADS * LLM_HD,), 0.5, 3.0, ((0, 4),), jnp.float32)
    return dict(enc_frames=enc_frames, span_counts=span_counts, enc_gain=enc_gain, enc_wq=enc_wq, enc_wk=enc_wk, enc_wv=enc_wv, enc_wo=enc_wo, adapter=adapter, owner_map=owner_map, text_embeds=text_embeds, llm_gain=llm_gain, llm_wq=llm_wq, llm_wk=llm_wk, llm_wv=llm_wv, llm_bq=llm_bq, llm_bk=llm_bk, llm_bv=llm_bv)


def layer_norm(samples, norm_gain):
    average = lax.optimization_barrier(jnp.mean(samples, axis=-1, keepdims=True))
    centred = samples - average
    variance = lax.optimization_barrier(jnp.mean(centred * centred, axis=-1, keepdims=True))
    return centred * lax.rsqrt(variance + 1e-05) * norm_gain

def root_norm(samples, norm_gain):
    power = lax.optimization_barrier(jnp.mean(samples * samples, axis=-1, keepdims=True))
    return samples * lax.rsqrt(power + 1e-06) * norm_gain

def rotate(vectors, positions):
    half_width = vectors.shape[-1] // 2
    inv_freq = jnp.exp(jnp.arange(half_width, dtype=jnp.float32) * (-2.0 * math.log(1000000.0) / vectors.shape[-1]))
    angles = positions.astype(jnp.float32)[:, None] * inv_freq[None, :]
    cosine = jnp.cos(angles)
    sine_table = jnp.sin(angles)
    lower_half = vectors[..., :half_width]
    upper_half = vectors[..., half_width:]
    return jnp.concatenate([lower_half * cosine - upper_half * sine_table, upper_half * cosine + lower_half * sine_table], axis=-1)

def span_attention(query_rows, key_rows, value_rows, key_open, head_width):
    frame_count = query_rows.shape[0]
    head_count = query_rows.shape[1] // head_width
    head_queries = query_rows.reshape(frame_count, head_count, head_width).transpose(1, 0, 2)
    head_keys = key_rows.reshape(-1, head_count, head_width).transpose(1, 0, 2)
    head_values = value_rows.reshape(-1, head_count, head_width).transpose(1, 0, 2)

    def one_head(operands):
        one_query, one_key, one_value = operands
        scores = jnp.dot(one_query, one_key.T, preferred_element_type=jnp.float32) * head_width ** (-0.5)
        scores = jnp.where(key_open[None, :], scores, -1e+30)
        peak = lax.optimization_barrier(jnp.max(scores, axis=-1, keepdims=True))
        weights = jnp.exp(scores - peak)
        probabilities = (weights / lax.optimization_barrier(jnp.sum(weights, axis=-1, keepdims=True))).astype(jnp.bfloat16)
        return jnp.dot(probabilities, one_value, preferred_element_type=jnp.float32).astype(jnp.bfloat16)
    context = lax.map(one_head, (head_queries, head_keys, head_values))
    return context.transpose(1, 0, 2).reshape(frame_count, head_count * head_width)

def grouped_attention(query_heads, key_heads, value_heads, row_present, positions):
    head_width = query_heads.shape[-1]
    row_count = query_heads.shape[1]
    kv_count = key_heads.shape[0]
    grouped = query_heads.reshape(kv_count, -1, row_count, head_width).astype(jnp.float32)
    scores = jnp.einsum('kgqd,ksd->kgqs', grouped, key_heads.astype(jnp.float32)) * head_width ** (-0.5)
    allowed = (row_present[None, :] > 0) & (positions[None, :] <= positions[:, None]) | jnp.eye(row_count, dtype=bool)
    scores = jnp.where(allowed[None, None], scores, -1e+30)
    peak = lax.optimization_barrier(jnp.max(scores, axis=-1, keepdims=True))
    weights = jnp.exp(scores - peak)
    probabilities = (weights / lax.optimization_barrier(jnp.sum(weights, axis=-1, keepdims=True))).astype(jnp.bfloat16)
    context = jnp.einsum('kgqs,ksd->kgqd', probabilities.astype(jnp.float32), value_heads.astype(jnp.float32))
    return context.reshape(-1, row_count, head_width)

def reference(enc_frames, span_counts, enc_gain, enc_wq, enc_wk, enc_wv, enc_wo, adapter, owner_map, text_embeds, llm_gain, llm_wq, llm_wk, llm_wv, llm_bq, llm_bk, llm_bv):
    frame_blocks = enc_frames.reshape(SPANS, FRAMES, D_ENC)

    def project(span_rows):
        normed = layer_norm(span_rows.astype(jnp.float32), enc_gain).astype(jnp.bfloat16)
        return (jnp.dot(normed, enc_wq, preferred_element_type=jnp.float32).astype(jnp.bfloat16), jnp.dot(normed, enc_wk, preferred_element_type=jnp.float32).astype(jnp.bfloat16), jnp.dot(normed, enc_wv, preferred_element_type=jnp.float32).astype(jnp.bfloat16))
    enc_query, enc_key, enc_value = lax.map(project, frame_blocks)
    prior_keys = jnp.concatenate([jnp.zeros_like(enc_key[:1]), enc_key[:-1]], axis=0)
    prior_values = jnp.concatenate([jnp.zeros_like(enc_value[:1]), enc_value[:-1]], axis=0)
    starts = (jnp.cumsum(span_counts) - span_counts).astype(jnp.int32)
    opening = jnp.any(starts[None, :] == jnp.arange(SPANS, dtype=jnp.int32)[:, None], axis=1)
    group_width = ENC_HEADS * ENC_HD // N_TENSOR

    def encode(operands):
        query_rows, key_rows, value_rows, prior_key, prior_value, opening_flag, span_rows = operands
        key_open = jnp.concatenate([jnp.broadcast_to(jnp.logical_not(opening_flag), (FRAMES,)), jnp.ones((FRAMES,), dtype=bool)])
        context = span_attention(query_rows, jnp.concatenate([prior_key, key_rows], axis=0), jnp.concatenate([prior_value, value_rows], axis=0), key_open, ENC_HD)
        summed_groups = jnp.zeros((POOLED, D_ENC), jnp.float32)
        for group_index in range(N_TENSOR):
            lower = group_index * group_width
            heads_out = jnp.dot(context[:, lower:lower + group_width], enc_wo[lower:lower + group_width], preferred_element_type=jnp.float32)
            pooled_part = (lax.optimization_barrier(jnp.sum(heads_out.reshape(POOLED, POOL, D_ENC), axis=1)) * (1.0 / POOL)).astype(jnp.bfloat16)
            summed_groups = summed_groups + lax.optimization_barrier(pooled_part).astype(jnp.float32)
        residual = lax.optimization_barrier(jnp.sum(span_rows.astype(jnp.float32).reshape(POOLED, POOL, D_ENC), axis=1)) * (1.0 / POOL)
        return (residual + summed_groups).astype(jnp.bfloat16)
    pooled = lax.map(encode, (enc_query, enc_key, enc_value, prior_keys, prior_values, opening, frame_blocks))
    pooled = pooled.reshape(SPANS * POOLED, D_ENC)
    adapted = jnp.dot(pooled, adapter, preferred_element_type=jnp.float32).astype(jnp.bfloat16)
    per_source = CH_DEV * POOLED
    owners = owner_map[:, 0].astype(jnp.int32)
    blocks = owners.reshape(N_TM, per_source)
    matches = (blocks[:, :, None] == jnp.arange(N_TM, dtype=jnp.int32)[None, None, :]).astype(jnp.int32)
    ordinal = lax.optimization_barrier(jnp.sum((jnp.cumsum(matches, axis=1) - 1) * matches, axis=2)).astype(jnp.int32).reshape(-1)
    sources = jnp.arange(SPANS * POOLED, dtype=jnp.int32) // per_source
    slot_index = (sources * SEND_CAP + ordinal).astype(jnp.int32)
    audio = jnp.zeros((N_TM, SLOTS, D_LLM), jnp.bfloat16).at[owners, slot_index].set(adapted)
    present = jnp.zeros((N_TM, SLOTS), jnp.int32).at[owners, slot_index].set(1)
    text_blocks = text_embeds.reshape(N_TM, TEXT, D_LLM)

    def decode(operands):
        audio_rows, audio_present, text_block = operands
        sequence = jnp.concatenate([audio_rows, text_block], axis=0)
        row_present = jnp.concatenate([audio_present, jnp.ones((TEXT,), jnp.int32)])
        positions = (jnp.cumsum(row_present) - 1).astype(jnp.int32)
        normed = root_norm(sequence.astype(jnp.float32), llm_gain).astype(jnp.bfloat16)
        query_proj = jnp.dot(normed, llm_wq, preferred_element_type=jnp.float32) + llm_bq
        key_proj = jnp.dot(normed, llm_wk, preferred_element_type=jnp.float32) + llm_bk
        value_proj = (jnp.dot(normed, llm_wv, preferred_element_type=jnp.float32) + llm_bv).astype(jnp.bfloat16)
        query_heads = rotate(query_proj.reshape(ROWS, Q_HEADS, LLM_HD).transpose(1, 0, 2), positions).astype(jnp.bfloat16)
        key_heads = rotate(key_proj.reshape(ROWS, KV_HEADS, LLM_HD).transpose(1, 0, 2), positions).astype(jnp.bfloat16)
        value_heads = value_proj.reshape(ROWS, KV_HEADS, LLM_HD).transpose(1, 0, 2)
        context_heads = grouped_attention(query_heads, key_heads, value_heads, row_present, positions)
        merged = context_heads.transpose(1, 0, 2).reshape(ROWS, Q_HEADS * LLM_HD)
        return (merged * row_present[:, None].astype(jnp.float32)).astype(jnp.bfloat16)
    output = lax.map(decode, (audio, present, text_blocks))
    return output.reshape(N_TM * ROWS, Q_HEADS * LLM_HD)
```

```python
import functools
import math

import jax
import jax.numpy as jnp
from jax import lax
from jax.experimental import pallas as pl
from jax.experimental.pallas import tpu as pltpu
from jax.sharding import PartitionSpec as P

B16 = jnp.bfloat16
F32 = jnp.float32
MESH = pl.DeviceIdType.MESH

ENC_HD = 64
FRAMES = 1500
POOL = 4
LLM_HD = 128
PAD = 1536
ROWS = 384
TILES = PAD // ROWS
PROWS = ROWS // POOL
POOLED = PAD // POOL
SLOT = 8
FEAT = 320
WIDE = 384
LOG2E = math.log2(math.e)


def dot(a, b):
    return jnp.dot(a, b, preferred_element_type=F32)


def encoder_kernel(
    n_tm,
    n_t,
    frames_ref,
    gain_ref,
    wq_ref,
    wk_ref,
    wv_ref,
    wo_ref,
    target_ref,
    open_ref,
    x_ref,
    tail_ref,
    q_ref,
    kt_ref,
    v_ref,
    ktp_ref,
    vp_ref,
    vm_ref,
    o1_ref,
    m1_ref,
    l1_ref,
    res_ref,
    part_ref,
    rs_ref,
    slots_ref,
    got_ref,
    kv_send,
    kv_recv,
    rs_send,
    rs_recv,
    a2a_send,
    a2a_recv,
    ag_send,
    ag_recv,
):
    me = lax.axis_index("tm")
    t = lax.axis_index("tensor")
    lane = lax.broadcasted_iota(jnp.int32, (1, 256), 1) // ENC_HD
    heads = 256 // ENC_HD

    barrier = pltpu.get_barrier_semaphore()

    def greet(k, _):
        pl.semaphore_signal(
            barrier, inc=1, device_id=(lax.rem(me + k, n_tm), t), device_id_type=MESH
        )
        return 0

    lax.fori_loop(1, n_tm, greet, 0)
    for k in range(1, n_t):
        pl.semaphore_signal(
            barrier, inc=1, device_id=(me, lax.rem(t + k, n_t)), device_id_type=MESH
        )

    tail_ref[...] = jnp.zeros_like(tail_ref)
    tail_ref[0 : FRAMES - 1280, :] = frames_ref[1280:FRAMES, :]
    prow = lax.broadcasted_iota(jnp.int32, (64, 256), 0)
    pcol = lax.broadcasted_iota(jnp.int32, (64, 256), 1)
    pool = jnp.where(pcol // POOL == prow, 0.25, 0.0).astype(B16)

    def project(raw, i):
        rows = pl.ds(pl.multiple_of(i * 256, 256), 256)
        x = raw.astype(F32)
        mean = jnp.mean(x, axis=-1, keepdims=True)
        cent = x - mean
        var = jnp.mean(cent * cent, axis=-1, keepdims=True)
        normed = (cent * lax.rsqrt(var + 1e-05) * gain_ref[...]).astype(B16)
        q_ref[rows, :] = (dot(normed, wq_ref[...]) * (ENC_HD**-0.5 * LOG2E)).astype(B16)
        kt_ref[:, rows] = jnp.transpose(dot(normed, wk_ref[...])).astype(B16)
        v_ref[rows, :] = dot(normed, wv_ref[...]).astype(B16)
        res = dot(pool, raw)
        prows = pl.ds(pl.multiple_of(i * 64, 64), 64)
        for tt in range(n_t):

            @pl.when(t == tt)
            def _():
                res_ref[prows, :] = res[:, tt * FEAT : (tt + 1) * FEAT]

    def project_block(i, _):
        project(frames_ref[pl.ds(pl.multiple_of(i * 256, 256), 256), :], i)
        return 0

    lax.fori_loop(0, 5, project_block, 0)
    project(tail_ref[...], 5)

    pl.semaphore_wait(barrier, n_tm - 1 + n_t - 1)

    def passed(src, dst, k):
        return pltpu.make_async_remote_copy(
            src_ref=src,
            dst_ref=dst,
            send_sem=kv_send.at[k],
            recv_sem=kv_recv.at[k],
            device_id=(lax.rem(me + 1, n_tm), t),
            device_id_type=MESH,
        )

    keys_on = passed(kt_ref, ktp_ref, 0)
    values_on = passed(v_ref, vp_ref, 1)
    keys_on.start()
    values_on.start()

    tail_lane = lax.broadcasted_iota(jnp.int32, (1, 128), 1) < FRAMES - (PAD - 128)

    def head_masks(values):
        for h in range(heads):
            vm_ref[h] = jnp.where(lane == h, values, jnp.ones((), B16))

    def half(rows, keys_ref):
        q = q_ref[rows, :]
        out = jnp.zeros((ROWS, 256), F32)
        top = jnp.zeros((ROWS, 256), F32)
        den = jnp.zeros((ROWS, 256), F32)
        for h in range(heads):
            s = dot(jnp.where(lane == h, q, jnp.zeros_like(q)), keys_ref[...])
            s = jnp.concatenate(
                [s[:, : PAD - 128], jnp.where(tail_lane, s[:, PAD - 128 :], -1e30)], axis=1
            )
            m = jnp.max(s, axis=1, keepdims=True)
            p = jnp.exp2(s - m).astype(B16)
            o = dot(p, vm_ref[h])
            col = 255 if h < heads - 1 else 0
            out = jnp.where(lane == h, o, out)
            top = jnp.where(lane == h, m, top)
            den = jnp.where(lane == h, o[:, col : col + 1], den)
        return out, top, den

    head_masks(v_ref[...])

    def own_half(i, _):
        rows = pl.ds(pl.multiple_of(i * ROWS, ROWS), ROWS)
        out, top, den = half(rows, kt_ref)
        o1_ref[rows, :] = out
        m1_ref[rows, :] = top
        l1_ref[rows, :] = den
        return 0

    lax.fori_loop(0, TILES, own_half, 0)

    keys_on.wait()
    values_on.wait()
    head_masks(vp_ref[...])
    is_open = open_ref[0, 0] > 0
    trow = lax.broadcasted_iota(jnp.int32, (PROWS, ROWS), 0)
    tcol = lax.broadcasted_iota(jnp.int32, (PROWS, ROWS), 1)
    tile_pool = jnp.where(tcol // POOL == trow, 0.25, 0.0).astype(B16)

    def summed(i, k):
        rows = pl.ds(pl.multiple_of(i * PROWS, PROWS), PROWS)
        to = lax.rem(t + k, n_t)
        return pltpu.make_async_remote_copy(
            src_ref=part_ref.at[to, rows],
            dst_ref=rs_ref.at[t, rows],
            send_sem=rs_send.at[i, k - 1],
            recv_sem=rs_recv.at[i, k - 1],
            device_id=(me, to),
            device_id_type=MESH,
        )

    def prior_half(i, _):
        rows = pl.ds(pl.multiple_of(i * ROWS, ROWS), ROWS)
        out, top, den = half(rows, ktp_ref)
        m1 = m1_ref[rows, :]
        both = jnp.where(is_open, m1, jnp.maximum(m1, top))
        w1 = jnp.exp2(m1 - both)
        w2 = jnp.where(is_open, 0.0, jnp.exp2(jnp.minimum(top - both, 0.0)))
        total = w1 * l1_ref[rows, :] + w2 * den
        ctx = ((w1 * o1_ref[rows, :] + w2 * out) / total).astype(B16)
        pooled = dot(tile_pool, ctx).astype(B16)
        partial = dot(pooled, wo_ref[...]).astype(B16)
        prows = pl.ds(pl.multiple_of(i * PROWS, PROWS), PROWS)
        for tt in range(n_t):
            part_ref[tt, prows, :] = partial[:, tt * FEAT : (tt + 1) * FEAT]
        for k in range(1, n_t):
            summed(i, k).start()
        return 0

    lax.fori_loop(0, TILES, prior_half, 0)

    def summed_wait(i, _):
        for k in range(1, n_t):
            summed(i, k).wait()
        return 0

    lax.fori_loop(0, TILES, summed_wait, 0)

    total = part_ref[t].astype(F32)
    for k in range(1, n_t):
        total = total + rs_ref[lax.rem(t + k, n_t)].astype(F32)
    pooled = (res_ref[...] + total).astype(B16)
    wide = jnp.concatenate([pooled, jnp.ones((POOLED, WIDE - FEAT), B16)], axis=1)
    slot_row = lax.broadcasted_iota(jnp.int32, (n_tm * SLOT, POOLED), 0)
    place = jnp.where(slot_row == target_ref[...], 1.0, 0.0).astype(B16)
    slots_ref[...] = dot(place, wide).reshape(n_tm, SLOT, WIDE).astype(B16)
    got_ref[me] = slots_ref[me]

    def routed(k):
        to = lax.rem(me + k, n_tm)
        return pltpu.make_async_remote_copy(
            src_ref=slots_ref.at[to],
            dst_ref=got_ref.at[me],
            send_sem=a2a_send,
            recv_sem=a2a_recv,
            device_id=(to, t),
            device_id_type=MESH,
        )

    def routed_start(k, _):
        routed(k).start()
        return 0

    lax.fori_loop(1, n_tm, routed_start, 0)
    many = slots_ref.at[pl.ds(0, n_tm - 1)]
    pltpu.make_async_copy(many, many, a2a_send).wait()
    many = got_ref.at[pl.ds(0, n_tm - 1)]
    pltpu.make_async_copy(many, many, a2a_recv).wait()

    def spread(k):
        return pltpu.make_async_remote_copy(
            src_ref=got_ref,
            dst_ref=x_ref.at[t],
            send_sem=ag_send.at[k - 1],
            recv_sem=ag_recv.at[k - 1],
            device_id=(me, lax.rem(t + k, n_t)),
            device_id_type=MESH,
        )

    for k in range(1, n_t):
        spread(k).start()
    x_ref[t] = got_ref[...]
    for k in range(1, n_t):
        spread(k).wait()


def run_encoder(n_tm, n_t, frames, gain, wq, wk, wv, wo, target, is_open):
    vmem = pl.BlockSpec(memory_space=pltpu.VMEM)
    smem = pl.BlockSpec(memory_space=pltpu.SMEM)
    return pl.pallas_call(
        functools.partial(encoder_kernel, n_tm, n_t),
        out_shape=jax.ShapeDtypeStruct((n_t, n_tm, SLOT, WIDE), B16),
        in_specs=[vmem] * 7 + [smem],
        out_specs=vmem,
        scratch_shapes=[
            pltpu.VMEM((256, frames.shape[1]), B16),
            pltpu.VMEM((PAD, 256), B16),
            pltpu.VMEM((256, PAD), B16),
            pltpu.VMEM((PAD, 256), B16),
            pltpu.VMEM((256, PAD), B16),
            pltpu.VMEM((PAD, 256), B16),
            pltpu.VMEM((256 // ENC_HD, PAD, 256), B16),
            pltpu.VMEM((PAD, 256), F32),
            pltpu.VMEM((PAD, 256), F32),
            pltpu.VMEM((PAD, 256), F32),
            pltpu.VMEM((POOLED, FEAT), F32),
            pltpu.VMEM((n_t, POOLED, FEAT), B16),
            pltpu.VMEM((n_t, POOLED, FEAT), B16),
            pltpu.VMEM((n_tm, SLOT, WIDE), B16),
            pltpu.VMEM((n_tm, SLOT, WIDE), B16),
            pltpu.SemaphoreType.DMA((2,)),
            pltpu.SemaphoreType.DMA((2,)),
            pltpu.SemaphoreType.DMA((TILES, n_t - 1)),
            pltpu.SemaphoreType.DMA((TILES, n_t - 1)),
            pltpu.SemaphoreType.DMA,
            pltpu.SemaphoreType.DMA,
            pltpu.SemaphoreType.DMA((n_t - 1,)),
            pltpu.SemaphoreType.DMA((n_t - 1,)),
        ],
        compiler_params=pltpu.CompilerParams(
            collective_id=0, has_side_effects=True, vmem_limit_bytes=56 << 20
        ),
        cost_estimate=pl.CostEstimate(
            flops=20_000_000_000, bytes_accessed=20_000_000, transcendentals=20_000_000
        ),
    )(frames, gain, wq, wk, wv, wo, target, is_open)


def root_norm(samples, norm_gain):
    power = jnp.mean(samples * samples, axis=-1, keepdims=True)
    return samples * lax.rsqrt(power + 1e-06) * norm_gain


def rotate(vectors, positions):
    half_width = vectors.shape[-1] // 2
    inv_freq = jnp.exp(
        jnp.arange(half_width, dtype=jnp.float32) * (-2.0 * math.log(1000000.0) / vectors.shape[-1])
    )
    angles = positions.astype(jnp.float32)[:, None] * inv_freq[None, :]
    cosine = jnp.cos(angles)
    sine_table = jnp.sin(angles)
    lower_half = vectors[..., :half_width]
    upper_half = vectors[..., half_width:]
    return jnp.concatenate(
        [
            lower_half * cosine - upper_half * sine_table,
            upper_half * cosine + lower_half * sine_table,
        ],
        axis=-1,
    )


def grouped_attention(query_heads, key_heads, value_heads, row_present, positions):
    head_width = query_heads.shape[-1]
    row_count = query_heads.shape[1]
    kv_count = key_heads.shape[0]
    grouped = query_heads.reshape(kv_count, -1, row_count, head_width)
    scores = jnp.einsum(
        "kgqd,ksd->kgqs", grouped, key_heads, preferred_element_type=jnp.float32
    ) * head_width ** (-0.5)
    allowed = (row_present[None, :] > 0) & (positions[None, :] <= positions[:, None]) | jnp.eye(
        row_count, dtype=bool
    )
    scores = jnp.where(allowed[None, None], scores, -1e30)
    peak = jnp.max(scores, axis=-1, keepdims=True)
    weights = jnp.exp(scores - peak)
    probabilities = (weights / jnp.sum(weights, axis=-1, keepdims=True)).astype(jnp.bfloat16)
    context = jnp.einsum(
        "kgqs,ksd->kgqd", probabilities, value_heads, preferred_element_type=jnp.float32
    )
    return context.reshape(-1, row_count, head_width)


def shards(
    enc_frames,
    span_counts,
    enc_gain,
    enc_wq,
    enc_wk,
    enc_wv,
    enc_wo,
    adapter,
    owner_map,
    text_embeds,
    llm_gain,
    llm_wq,
    llm_wk,
    llm_wv,
    llm_bq,
    llm_bk,
    llm_bv,
):
    n_tm = lax.axis_size("tm")
    n_t = lax.axis_size("tensor")
    me = lax.axis_index("tm")
    count = FRAMES // POOL
    starts = jnp.cumsum(span_counts) - span_counts
    is_open = jnp.any(starts == me).astype(jnp.int32).reshape(1, 1)
    own = lax.dynamic_slice_in_dim(owner_map, me * count, count, 0)[:, 0]
    order = jnp.arange(count, dtype=jnp.int32)
    earlier = (own[:, None] == own[None, :]) & (order[:, None] < order[None, :])
    ordinal = jnp.sum(earlier.astype(jnp.int32), axis=0)
    target = jnp.pad(own * SLOT + ordinal, (0, POOLED - count), constant_values=-1)[None, :]
    weight = lax.all_gather(
        jnp.concatenate([llm_wq, llm_wk, llm_wv], axis=1), "tm", axis=0, tiled=True
    )
    x4 = run_encoder(
        n_tm, n_t, enc_frames, enc_gain[None, :], enc_wq, enc_wk, enc_wv, enc_wo, target, is_open
    )
    used = SLOT - 1
    filled = (x4[0, :, :used, FEAT] > 0).astype(jnp.int32).reshape(-1)
    pooled = (
        x4[:, :, :used, :FEAT].transpose(1, 2, 0, 3).reshape(n_tm * used, n_t * FEAT)
    )
    adapted = jnp.dot(pooled, adapter, preferred_element_type=jnp.float32).astype(jnp.bfloat16)
    audio = lax.all_gather(adapted, "tensor", axis=1, tiled=True)
    sequence = jnp.concatenate([audio, text_embeds], axis=0)
    row_count = sequence.shape[0]
    row_present = jnp.concatenate([filled, jnp.ones((text_embeds.shape[0],), jnp.int32)])
    positions = jnp.cumsum(row_present) - 1
    seq_normed = root_norm(sequence.astype(jnp.float32), llm_gain).astype(jnp.bfloat16)
    proj = jnp.dot(seq_normed, weight, preferred_element_type=jnp.float32)
    nq = llm_bq.shape[0]
    nk = llm_bk.shape[0]
    query_heads = rotate(
        (proj[:, :nq] + llm_bq).reshape(row_count, -1, LLM_HD).transpose(1, 0, 2), positions
    ).astype(jnp.bfloat16)
    key_heads = rotate(
        (proj[:, nq : nq + nk] + llm_bk).reshape(row_count, -1, LLM_HD).transpose(1, 0, 2),
        positions,
    ).astype(jnp.bfloat16)
    value_heads = (
        (proj[:, nq + nk :] + llm_bv)
        .astype(jnp.bfloat16)
        .reshape(row_count, -1, LLM_HD)
        .transpose(1, 0, 2)
    )
    context_heads = grouped_attention(query_heads, key_heads, value_heads, row_present, positions)
    merged = context_heads.transpose(1, 0, 2).reshape(row_count, -1)
    return (merged * row_present[:, None].astype(jnp.float32)).astype(jnp.bfloat16)


def solution(mesh):
    placed = (
        P("tm", None),
        P(),
        P(),
        P(None, "tensor"),
        P(None, "tensor"),
        P(None, "tensor"),
        P("tensor", None),
        P(None, "tensor"),
        P(),
        P("tm", None),
        P(),
        P("tm", "tensor"),
        P("tm", "tensor"),
        P("tm", "tensor"),
        P("tensor"),
        P("tensor"),
        P("tensor"),
    )
    return jax.shard_map(
        shards, mesh=mesh, in_specs=placed, out_specs=P("tm", "tensor"), check_vma=False
    )
```

```python
import functools
import math
import types

import jax
import jax.numpy as jnp
import numpy as np
from jax import lax
from jax.experimental import pallas as pl
from jax.experimental.pallas import tpu as pltpu
from jax.sharding import PartitionSpec as P

B16 = jnp.bfloat16
F32 = jnp.float32
MESH = pl.DeviceIdType.MESH

ENC_HD = 64
FRAMES = 1500
POOL = 4
LLM_HD = 128
PAD = 1536
ROWS = 384
TILES = PAD // ROWS
PROWS = ROWS // POOL
PART = PAD // 2
POOLED = PAD // POOL
SLOT = 8
FEAT = 320
WIDE = 384
LOG2E = math.log2(math.e)
NX = 4
NZ = 8
NC = 2
D_LLM = 3584
SEQ = 512
CHUNK = 56
PIECE = NC * CHUNK
BLOCK = 256
AROWS = 80
QKV = 1152


def dot(a, b):
    return jnp.dot(a, b, preferred_element_type=F32)


INPUTS = ("frames", "wq", "wk", "wv", "adapter", "wo", "text", "rope")
SMALL = ("gain", "owners", "counts", "llm_gain", "pq", "pk", "pv", "bq", "bk", "bv")
HBM, SEND, RECV = "hbm_", "_send", "_recv"
GROUPS = 4


def block_kernel(n_tm, n_t, names, *refs):
    r = types.SimpleNamespace(**dict(zip(names, refs, strict=True)))
    me = lax.axis_index("tm")
    t = lax.axis_index("tensor")
    z = me // (NX * NC)
    xx = lax.rem(me // NC, NX)
    c = lax.rem(me, NC)
    lane = lax.broadcasted_iota(jnp.int32, (1, 256), 1) // ENC_HD
    heads = 256 // ENC_HD

    def at(zz, xv, cv):
        return ((zz * NX + xv) * NC + cv, t)

    def x_other(k):
        return lax.rem(xx + k, NX)

    def t_other(k):
        return lax.rem(t + k, n_t)

    mate = at(z, xx, 1 - c)

    def remote(src, dst, send, recv, to):
        return pltpu.make_async_remote_copy(
            src_ref=src, dst_ref=dst, send_sem=send, recv_sem=recv, device_id=to, device_id_type=MESH
        )

    def drain(ref, sem):
        pltpu.make_async_copy(ref, ref, sem).wait()

    barrier = pltpu.get_barrier_semaphore()

    def greet(k, _):
        pl.semaphore_signal(
            barrier, inc=1, device_id=(lax.rem(me + k, n_tm), t), device_id_type=MESH
        )
        return 0

    lax.fori_loop(1, n_tm, greet, 0)
    for k in range(1, n_t):
        pl.semaphore_signal(barrier, inc=1, device_id=(me, t_other(k)), device_id_type=MESH)

    def fetched(name):
        return pltpu.make_async_copy(
            getattr(r, HBM + name), getattr(r, name), r.in_sem.at[INPUTS.index(name)]
        )

    for name in INPUTS:
        fetched(name).start()

    cut = 640

    def ring(k):
        return lax.rem(z + NZ + k, NZ)

    def ring_sent(buf, sems, k, to, step, cols=None):
        ref = buf.at[c, ring(k)]
        if cols is not None:
            ref = buf.at[c, ring(k), :, cols]
        remote(
            ref, ref, getattr(r, sems + SEND), getattr(r, sems + RECV).at[step], at(ring(to), xx, c)
        ).start()

    def to_mate(buf, sems, k):
        ref = buf.at[c, ring(k)]
        remote(ref, ref, getattr(r, sems + SEND), getattr(r, sems + RECV), mate).start()

    def ring_first(buf, sems):
        for k in (2, -2, 1, -1):
            ring_sent(buf, sems, 0, k, 0)

    def ring_second(buf, sems, mate_sems):
        drain(buf.at[c, pl.ds(0, 4)], getattr(r, sems + RECV).at[0])
        ring_sent(buf, sems, -2, 2, 1, slice(0, cut))
        ring_sent(buf, sems, 2, -2, 1, slice(cut, QKV))
        ring_sent(buf, sems, -2, 1, 1)
        ring_sent(buf, sems, 2, -1, 1)
        for k in (0, 1, -1, 2, -2):
            to_mate(buf, mate_sems, k)

    def ring_last(buf, sems, mate_sems):
        drain(buf.at[c, pl.ds(0, 3)], getattr(r, sems + RECV).at[1])
        for k in (3, -3, 4):
            to_mate(buf, mate_sems, k)

    def ring_done(buf, sems, mate_sems):
        drain(buf.at[c, pl.ds(0, NZ - 1)], getattr(r, sems + SEND))
        drain(buf.at[c], getattr(r, mate_sems + SEND))
        drain(buf.at[1 - c], getattr(r, mate_sems + RECV))

    nq, nk = r.pq.shape[1], r.pk.shape[1]
    own_w = r.wz.at[c, z]
    own_w[:, :nq] = r.pq[...]
    own_w[:, nq : nq + nk] = r.pk[...]
    own_w[:, nq + nk :] = r.pv[...]

    def adapter_rows(k):
        return remote(
            r.asel.at[xx],
            r.arow.at[t],
            r.as_send.at[k - 1],
            r.as_recv.at[k - 1],
            (me, t_other(k)),
        )

    def text_rows(k):
        xv = x_other(k)
        return remote(
            r.tp.at[xv],
            r.trow.at[xx],
            r.tp_send.at[k - 1],
            r.tp_recv.at[k - 1],
            at(z, xv, c),
        )

    for name in ("frames", "wq", "wk", "wv"):
        fetched(name).wait()
    tail_ref, frames_ref = r.tail, r.frames
    gain = r.gain[...].reshape(1, -1)
    tail_ref[...] = jnp.zeros_like(tail_ref)
    tail_ref[0 : FRAMES - 1280, :] = frames_ref[1280:FRAMES, :]
    prow = lax.broadcasted_iota(jnp.int32, (64, 256), 0)
    pcol = lax.broadcasted_iota(jnp.int32, (64, 256), 1)
    pool = jnp.where(pcol // POOL == prow, 0.25, 0.0).astype(B16)

    def project(raw, i):
        rows = pl.ds(pl.multiple_of(i * 256, 256), 256)
        x = raw.astype(F32)
        mean = jnp.mean(x, axis=-1, keepdims=True)
        cent = x - mean
        var = jnp.mean(cent * cent, axis=-1, keepdims=True)
        normed = (cent * lax.rsqrt(var + 1e-05) * gain).astype(B16)
        r.q[rows, :] = (dot(normed, r.wq[...]) * (ENC_HD**-0.5 * LOG2E)).astype(B16)
        r.kt[:, rows] = jnp.transpose(dot(normed, r.wk[...])).astype(B16)
        r.v[rows, :] = dot(normed, r.wv[...]).astype(B16)
        res = dot(pool, raw)
        prows = pl.ds(pl.multiple_of(i * 64, 64), 64)
        for tt in range(n_t):

            @pl.when(t == tt)
            def _():
                r.res[prows, :] = res[:, tt * FEAT : (tt + 1) * FEAT]

    def project_block(i, _):
        project(frames_ref[pl.ds(pl.multiple_of(i * 256, 256), 256), :], i)
        return 0

    lax.fori_loop(0, 5, project_block, 0)
    project(tail_ref[...], 5)

    pl.semaphore_wait(barrier, n_tm - 1 + n_t - 1)
    ring_first(r.wz, "wz")

    onward = (lax.rem(me + 1, n_tm), t)

    def keys_on(part):
        cols = slice(part * PART, (part + 1) * PART)
        i = 2 * part
        return (
            remote(r.kt.at[:, cols], r.ktp.at[:, cols], r.kv_send.at[i], r.kv_recv.at[i], onward),
            remote(r.v.at[cols], r.vp.at[cols], r.kv_send.at[i + 1], r.kv_recv.at[i + 1], onward),
        )

    for part in range(2):
        for copy in keys_on(part):
            copy.start()

    fetched("adapter").wait()
    width = r.adapter.shape[1]
    llm_gain = r.llm_gain[...].reshape(1, -1)
    r.asel[...] = jnp.zeros_like(r.asel)
    r.gp[...] = jnp.zeros_like(r.gp)
    own_a = r.adapter[pl.ds(pl.multiple_of((c * NZ + z) * AROWS, AROWS), AROWS), :]
    for xv in range(NX):
        for zz in range(2):
            lo = zz * NX * PIECE + xv * PIECE
            r.asel[xv, :, zz * PIECE : (zz + 1) * PIECE] = own_a[:, lo : lo + PIECE]
            for tt in range(n_t):
                to = tt * BLOCK + zz * PIECE
                r.gp[xv, 0:1, to : to + PIECE] = llm_gain[:, tt * width + lo : tt * width + lo + PIECE]
    r.arow[t] = r.asel[xx]
    for k in range(1, n_t):
        adapter_rows(k).start()

    tail_lane = lax.broadcasted_iota(jnp.int32, (1, 128), 1) < FRAMES - (PAD - 128)

    def head_masks(values_ref, lo, size):
        for h in range(heads):
            r.vm[h, lo : lo + size] = jnp.where(
                lane == h, values_ref[lo : lo + size, :], jnp.ones((), B16)
            )

    def attend(rows, keys_ref, lo, size):
        q = r.q[rows, :]
        out = jnp.zeros((ROWS, 256), F32)
        top = jnp.zeros((ROWS, 256), F32)
        den = jnp.zeros((ROWS, 256), F32)
        for h in range(heads):
            s = dot(jnp.where(lane == h, q, jnp.zeros_like(q)), keys_ref[:, lo : lo + size])
            if lo + size == PAD:
                end = jnp.where(tail_lane, s[:, size - 128 :], -1e30)
                s = jnp.concatenate([s[:, : size - 128], end], axis=1)
            m = jnp.max(s, axis=1, keepdims=True)
            p = jnp.exp2(s - m).astype(B16)
            o = dot(p, r.vm[h, lo : lo + size])
            col = 255 if h < heads - 1 else 0
            out = jnp.where(lane == h, o, out)
            top = jnp.where(lane == h, m, top)
            den = jnp.where(lane == h, o[:, col : col + 1], den)
        return out, top, den

    head_masks(r.v, 0, PAD)

    def own_half(i, _):
        @pl.when(i == TILES - 1)
        def _():
            ring_second(r.wz, "wz", "wm")

        rows = pl.ds(pl.multiple_of(i * ROWS, ROWS), ROWS)
        out, top, den = attend(rows, r.kt, 0, PAD)
        r.o1[rows, :] = out
        r.m1[rows, :] = top
        r.l1[rows, :] = den
        return 0

    lax.fori_loop(0, TILES, own_half, 0)

    fetched("text").wait()
    text = r.text[...].astype(F32)
    power = jnp.mean(text * text, axis=-1, keepdims=True)
    text = (text * lax.rsqrt(power + 1e-06) * llm_gain).astype(B16)
    r.tp[...] = jnp.zeros_like(r.tp)
    for xv in range(NX):
        for tt in range(n_t):
            for zz in range(2):
                lo = tt * width + zz * NX * PIECE + xv * PIECE
                to = tt * BLOCK + zz * PIECE
                r.tp[xv, :, to : to + PIECE] = text[:, lo : lo + PIECE]
    r.trow[xx] = r.tp[xx]
    def fused_sent(k):
        return remote(
            r.fx.at[xx],
            r.fx.at[xx],
            r.fx_send.at[k - 1],
            r.fx_recv.at[k - 1],
            at(z, x_other(k), c),
        )

    def text_sent(k):
        xv = x_other(k)
        return remote(
            r.tsend.at[xv],
            r.trecv.at[xx],
            r.tx_send.at[k - 1],
            r.tx_recv.at[k - 1],
            at(z, xv, c),
        )

    def multiply_slab():
        ring_done(r.wz, "wz", "wm")
        for k in range(1, n_t):
            adapter_rows(k).wait()
        for tt in range(n_t):
            rows = [
                r.wz[cv, 2 * tt + zz].astype(F32) for zz in range(2) for cv in range(NC)
            ]
            rows.append(jnp.zeros((BLOCK - 2 * PIECE, QKV), F32))
            r.wslab[tt * BLOCK : (tt + 1) * BLOCK, :] = jnp.concatenate(rows, axis=0).astype(B16)
        fused = jnp.zeros((AROWS, QKV), F32)
        gains = r.gp[xx]
        for tt in range(n_t):
            cols = slice(tt * BLOCK, (tt + 1) * BLOCK)
            scaled = (r.arow[tt].astype(F32) * gains[0:1, cols]).astype(B16)
            fused = fused + dot(scaled, r.wslab[cols, :])
        r.fx[xx] = fused.astype(B16)
        for k in range(1, NX):
            fused_sent(k).start()

    def multiply_text():
        for k in range(1, NX):
            text_rows(k).wait()
        for xv in range(NX):
            r.tsend[xv] = dot(r.trow[xv], r.wslab[...]).astype(B16)
        r.trecv[xx] = r.tsend[xx]
        for k in range(1, NX):
            text_sent(k).start()

    def spread_fused():
        for k in range(1, NX):
            fused_sent(k).wait()
        total = r.fx[0].astype(F32)
        for xv in range(1, NX):
            total = total + r.fx[xv].astype(F32)
        r.fall[c, z] = total.astype(B16)
        ring_first(r.fall, "fz")
        for k in range(1, NX):
            text_rows(k).start()

    for copy in keys_on(0):
        copy.wait()
    head_masks(r.vp, 0, PART)
    fetched("wo").wait()
    begin = jnp.int32(0)
    openings = jnp.int32(0)
    for i in range(r.counts.shape[0]):
        openings = openings + jnp.where(begin == me, 1, 0)
        begin = begin + r.counts[i]
    is_open = openings > 0
    trow = lax.broadcasted_iota(jnp.int32, (PROWS, ROWS), 0)
    tcol = lax.broadcasted_iota(jnp.int32, (PROWS, ROWS), 1)
    tile_pool = jnp.where(tcol // POOL == trow, 0.25, 0.0).astype(B16)

    def summed(i, k):
        rows = pl.ds(pl.multiple_of(i * PROWS, PROWS), PROWS)
        to = t_other(k)
        return remote(
            r.part.at[to, rows],
            r.rs.at[t, rows],
            r.rs_send.at[i, k - 1],
            r.rs_recv.at[i, k - 1],
            (me, to),
        )

    def merged(rows, lo):
        out, top, den = attend(rows, r.ktp, lo, PART)
        m1 = r.m1[rows, :]
        both = jnp.where(is_open, m1, jnp.maximum(m1, top))
        w1 = jnp.exp2(m1 - both)
        w2 = jnp.where(is_open, 0.0, jnp.exp2(jnp.minimum(top - both, 0.0)))
        return w1 * r.o1[rows, :] + w2 * out, both, w1 * r.l1[rows, :] + w2 * den

    def prior_first(i, _):
        @pl.when(i == 1)
        def _():
            ring_last(r.wz, "wz", "wm")

        @pl.when(i == TILES - 1)
        def _():
            multiply_slab()

        rows = pl.ds(pl.multiple_of(i * ROWS, ROWS), ROWS)
        out, top, den = merged(rows, 0)
        r.o1[rows, :] = out
        r.m1[rows, :] = top
        r.l1[rows, :] = den
        return 0

    lax.fori_loop(0, TILES, prior_first, 0)

    for copy in keys_on(1):
        copy.wait()
    head_masks(r.vp, PART, PART)

    def prior_second(i, _):
        @pl.when(i == TILES - 1)
        def _():
            spread_fused()

        rows = pl.ds(pl.multiple_of(i * ROWS, ROWS), ROWS)
        out, top, den = merged(rows, PART)
        ctx = (out / den).astype(B16)
        pooled = dot(tile_pool, ctx).astype(B16)
        partial = dot(pooled, r.wo[...]).astype(B16)
        prows = pl.ds(pl.multiple_of(i * PROWS, PROWS), PROWS)
        for tt in range(n_t):
            r.part[tt, prows, :] = partial[:, tt * FEAT : (tt + 1) * FEAT]
        for k in range(1, n_t):
            summed(i, k).start()
        return 0

    lax.fori_loop(0, TILES, prior_second, 0)

    def summed_wait(i, _):
        for k in range(1, n_t):
            summed(i, k).wait()
        return 0

    lax.fori_loop(0, TILES, summed_wait, 0)

    total = r.part[t].astype(F32)
    for k in range(1, n_t):
        total = total + r.rs[t_other(k)].astype(F32)
    pooled = (r.res[...] + total).astype(B16)
    wide = jnp.concatenate([pooled, jnp.ones((POOLED, WIDE - FEAT), B16)], axis=1)
    owners = jnp.broadcast_to(r.owners[...].astype(F32), (128, POOLED))
    same = jnp.transpose(owners)[:, 0:1] == owners[0:1, :]
    first = lax.broadcasted_iota(jnp.int32, (POOLED, POOLED), 0)
    then = lax.broadcasted_iota(jnp.int32, (POOLED, POOLED), 1)
    ordinal = jnp.sum(jnp.where(same & (first < then), 1.0, 0.0), axis=0, keepdims=True)
    target = owners[0:1, :] * SLOT + ordinal
    slot_row = lax.broadcasted_iota(jnp.int32, (n_tm * SLOT, POOLED), 0)
    place = jnp.where(slot_row.astype(F32) == target, 1.0, 0.0).astype(B16)
    slots_ref, x_ref = r.slots, r.x
    slots_ref[...] = dot(place, wide).reshape(n_tm, SLOT, WIDE).astype(B16)
    x_ref[t, 0] = slots_ref[me]
    members = n_tm // GROUPS

    for g in range(GROUPS):

        def routed_start(k, _, g=g):
            to = lax.rem(me + k, n_tm)
            remote(
                slots_ref.at[to], x_ref.at[t, k], r.a2a_send, r.a2a_recv.at[g], (to, t)
            ).start()
            return 0

        lax.fori_loop(max(1, g * members), (g + 1) * members, routed_start, 0)

    multiply_text()

    def handed(g, k):
        rows = pl.ds(g * members, members)
        ref = x_ref.at[t, rows]
        i = (k + 1) // 2
        return remote(
            ref, ref, r.ag_send.at[g, i], r.ag_recv.at[g, i], (me, lax.rem(t + n_t + k, n_t))
        )

    def relayed(g, k):
        part = members // 2
        rows = pl.ds(g * members + (0 if k > 0 else part), part)
        ref = x_ref.at[lax.rem(t + n_t - k, n_t), rows]
        i = (k + 1) // 2
        return remote(
            ref, ref, r.ar_send.at[g, i], r.ar_recv.at[g, i], (me, lax.rem(t + n_t + k, n_t))
        )

    def relay(g):
        for k in (1, -1):
            handed(g, k).wait()
        for k in (1, -1):
            relayed(g, k).start()

    for g in range(GROUPS):
        start = max(1, g * members)
        drain(x_ref.at[t, pl.ds(start, (g + 1) * members - start)], r.a2a_recv.at[g])
        for k in (1, -1):
            handed(g, k).start()
        if g == 1:
            ring_second(r.fall, "fz", "fm")
        if g > 0:
            relay(g - 1)
    relay(GROUPS - 1)
    drain(slots_ref.at[pl.ds(0, n_tm - 1)], r.a2a_send)
    for k in range(1, NX):
        text_sent(k).wait()
    for g in range(GROUPS):
        for k in (1, -1):
            relayed(g, k).wait()

    used = SLOT - 1
    audio = n_tm * used
    fetched("rope").wait()
    srow = lax.broadcasted_iota(jnp.int32, (audio, n_tm * SLOT), 0)
    scol = lax.broadcasted_iota(jnp.int32, (audio, n_tm * SLOT), 1)
    source = (me - (scol >> 3)) & (n_tm - 1)
    place = source * used + (scol & (SLOT - 1))
    compact = jnp.where((place == srow) & ((scol & (SLOT - 1)) < used), 1.0, 0.0).astype(B16)
    flags = None
    for tt in range(n_t):
        rows = x_ref[tt].astype(F32).reshape(n_tm * SLOT, WIDE).astype(B16)
        rows = dot(compact, rows)
        r.xc[:, tt * FEAT : (tt + 1) * FEAT] = rows[:, :FEAT].astype(B16)
        if tt == 0:
            flags = rows[:, FEAT : FEAT + 1]

    adapted = dot(r.xc[...], r.adapter[...])
    power = jnp.sum(adapted * adapted, axis=1, keepdims=True)
    power = jnp.concatenate([power, jnp.zeros((SEQ - audio, 1), F32)], axis=0)
    power = jnp.transpose(jnp.broadcast_to(power, (SEQ, 128)))
    r.ss[t] = power[0:8, :]

    def power_sent(k):
        return remote(
            r.ss.at[t], r.ss.at[t], r.ss_send.at[k - 1], r.ss_recv.at[k - 1], (me, t_other(k))
        )

    for k in range(1, n_t):
        power_sent(k).start()

    present = jnp.concatenate([flags, jnp.ones((SEQ - audio, 1), F32)], axis=0)
    present = jnp.broadcast_to(present, (SEQ, 128))
    row = lax.broadcasted_iota(jnp.int32, (SEQ, SEQ), 0)
    col = lax.broadcasted_iota(jnp.int32, (SEQ, SEQ), 1)
    until = jnp.where(col <= row, 1.0, 0.0).astype(B16)
    position = dot(until, present.astype(B16)) - 1.0
    chosen = jnp.where(col.astype(F32) == position[:, 0:1], 1.0, 0.0).astype(B16)
    high = r.rope[...].astype(B16)
    table = dot(chosen, high) + dot(chosen, (r.rope[...] - high.astype(F32)).astype(B16))
    cosine, sine = table[:, :LLM_HD], table[:, LLM_HD:]
    key_there = jnp.transpose(present)[0:1, :] > 0.5
    r.mask[...] = jnp.where(((col <= row) & key_there) | (col == row), 0.0, -1e30)

    ring_last(r.fall, "fz", "fm")
    ring_done(r.fall, "fz", "fm")
    r.qkv[0:audio, :] = dot(r.xc[...], r.fall[...].reshape(NC * NZ * AROWS, QKV))
    text_part = r.trecv[0].astype(F32)
    for xv in range(1, NX):
        text_part = text_part + r.trecv[xv].astype(F32)
    r.qkv[audio:SEQ, :] = text_part

    for k in range(1, n_t):
        power_sent(k).wait()
    power = r.ss[0]
    for tt in range(1, n_t):
        power = power + r.ss[tt]
    power = jnp.transpose(jnp.broadcast_to(power[0:1, :], (128, SEQ)))
    scale = lax.rsqrt(power * (1.0 / D_LLM) + 1e-06)
    row_of = lax.broadcasted_iota(jnp.int32, (SEQ, 128), 0)
    scale = jnp.where(row_of < audio, scale, 1.0)

    q_bias = r.bq[...].reshape(1, -1)

    def columns(i, bias):
        cols = slice(i * LLM_HD, (i + 1) * LLM_HD)
        return r.qkv[:, cols] * scale + bias

    def rotated(x):
        return x * cosine + pltpu.roll(x, LLM_HD // 2, 1) * sine

    q_heads = nq // LLM_HD
    keys = jnp.transpose(rotated(columns(q_heads, r.bk[...].reshape(1, -1)))).astype(B16)
    values = columns(q_heads + 1, r.bv[...].reshape(1, -1)).astype(B16)
    values = jnp.concatenate([values, jnp.ones((SEQ, LLM_HD), B16)], axis=1)
    for h in range(q_heads):
        bias = q_bias[:, h * LLM_HD : (h + 1) * LLM_HD]
        query = (rotated(columns(h, bias)) * (LLM_HD**-0.5 * LOG2E)).astype(B16)
        for lo in range(0, SEQ, 256):
            rows, end = slice(lo, lo + 256), lo + 256
            s = dot(query[rows], keys[:, :end]) + r.mask[rows, :end]
            m = jnp.max(s, axis=1, keepdims=True)
            o = dot(jnp.exp2(s - m).astype(B16), values[:end])
            ctx = o[:, :LLM_HD] / o[:, LLM_HD:] * present[rows]
            r.out[rows, h * LLM_HD : (h + 1) * LLM_HD] = ctx.astype(B16)


def rope_table():
    half = LLM_HD // 2
    freq = np.exp(
        np.arange(half, dtype=np.float32) * np.float32(-2.0 * math.log(1000000.0) / LLM_HD)
    ).astype(np.float32)
    angles = np.arange(SEQ, dtype=np.float32)[:, None] * freq[None, :]
    cosine = np.cos(angles.astype(np.float64)).astype(np.float32)
    sine = np.sin(angles.astype(np.float64)).astype(np.float32)
    return np.concatenate([cosine, cosine, -sine, sine], axis=1)


def run_block(n_tm, n_t, *args):
    vmem = pl.BlockSpec(memory_space=pltpu.VMEM)
    smem = pl.BlockSpec(memory_space=pltpu.SMEM)
    dma = pltpu.SemaphoreType.DMA
    audio = n_tm * (SLOT - 1)
    scratch = dict(
        tail=((256, 1280), B16),
        q=((PAD, 256), B16),
        kt=((256, PAD), B16),
        v=((PAD, 256), B16),
        ktp=((256, PAD), B16),
        vp=((PAD, 256), B16),
        vm=((256 // ENC_HD, PAD, 256), B16),
        o1=((PAD, 256), F32),
        m1=((PAD, 256), F32),
        l1=((PAD, 256), F32),
        res=((POOLED, FEAT), F32),
        part=((n_t, POOLED, FEAT), B16),
        rs=((n_t, POOLED, FEAT), B16),
        slots=((n_tm, SLOT, WIDE), B16),
        x=((n_t, n_tm, SLOT, WIDE), B16),
        wz=((NC, NZ, CHUNK, QKV), B16),
        wslab=((n_t * BLOCK, QKV), B16),
        tp=((NX, SEQ - audio, n_t * BLOCK), B16),
        gp=((NX, 8, n_t * BLOCK), F32),
        asel=((NX, AROWS, BLOCK), B16),
        arow=((n_t, AROWS, BLOCK), B16),
        trow=((NX, SEQ - audio, n_t * BLOCK), B16),
        tsend=((NX, SEQ - audio, QKV), B16),
        trecv=((NX, SEQ - audio, QKV), B16),
        fx=((NX, AROWS, QKV), B16),
        fall=((NC, NZ, AROWS, QKV), B16),
        xc=((audio, n_t * FEAT), B16),
        ss=((n_t, 8, SEQ), F32),
        qkv=((SEQ, QKV), F32),
        mask=((SEQ, SEQ), F32),
    )
    sems = dict(
        in_sem=(len(INPUTS),),
        kv_send=(4,),
        kv_recv=(4,),
        rs_send=(TILES, n_t - 1),
        rs_recv=(TILES, n_t - 1),
        a2a_send=(),
        a2a_recv=(GROUPS,),
        ag_send=(GROUPS, 2),
        ag_recv=(GROUPS, 2),
        ar_send=(GROUPS, 2),
        ar_recv=(GROUPS, 2),
        wz_send=(),
        wz_recv=(2,),
        wm_send=(),
        wm_recv=(),
        as_send=(n_t - 1,),
        as_recv=(n_t - 1,),
        tp_send=(NX - 1,),
        tp_recv=(NX - 1,),
        fx_send=(NX - 1,),
        fx_recv=(NX - 1,),
        tx_send=(NX - 1,),
        tx_recv=(NX - 1,),
        fz_send=(),
        fz_recv=(2,),
        fm_send=(),
        fm_recv=(),
        ss_send=(n_t - 1,),
        ss_recv=(n_t - 1,),
    )
    held = {n: (a.shape, a.dtype) for n, a in zip(INPUTS, args, strict=False)} | scratch
    shapes = [pltpu.VMEM(*a) for a in held.values()]
    shapes += [dma(a) if a else dma for a in sems.values()]
    names = [HBM + n for n in INPUTS] + [*SMALL, "out", *held, *sems]
    return pl.pallas_call(
        functools.partial(block_kernel, n_tm, n_t, names),
        out_shape=jax.ShapeDtypeStruct((SEQ, args[len(INPUTS) + SMALL.index("pq")].shape[1]), B16),
        in_specs=[pl.BlockSpec(memory_space=pl.ANY)] * len(INPUTS)
        + [smem if n == "counts" else vmem for n in SMALL],
        out_specs=vmem,
        scratch_shapes=shapes,
        compiler_params=pltpu.CompilerParams(
            collective_id=0, has_side_effects=True, vmem_limit_bytes=62 << 20
        ),
        cost_estimate=pl.CostEstimate(
            flops=20_000_000_000, bytes_accessed=20_000_000, transcendentals=20_000_000
        ),
    )(*args)


def shards(
    enc_frames,
    span_counts,
    enc_gain,
    enc_wq,
    enc_wk,
    enc_wv,
    enc_wo,
    adapter,
    owner_map,
    text_embeds,
    llm_gain,
    llm_wq,
    llm_wk,
    llm_wv,
    llm_bq,
    llm_bk,
    llm_bv,
):
    n_tm = lax.axis_size("tm")
    n_t = lax.axis_size("tensor")
    me = lax.axis_index("tm")
    count = FRAMES // POOL
    owners = lax.dynamic_slice_in_dim(owner_map, me * count, count, 0)[:, 0]
    owners = jnp.pad(owners, (0, POOLED - count), constant_values=-n_tm)[None, :]
    return run_block(
        n_tm,
        n_t,
        enc_frames,
        enc_wq,
        enc_wk,
        enc_wv,
        adapter,
        enc_wo,
        text_embeds,
        jnp.asarray(rope_table()),
        enc_gain,
        owners,
        span_counts,
        llm_gain,
        llm_wq,
        llm_wk,
        llm_wv,
        llm_bq,
        llm_bk,
        llm_bv,
    )


def solution(mesh):
    placed = (
        P("tm", None),
        P(),
        P(),
        P(None, "tensor"),
        P(None, "tensor"),
        P(None, "tensor"),
        P("tensor", None),
        P(None, "tensor"),
        P(),
        P("tm", None),
        P(),
        P("tm", "tensor"),
        P("tm", "tensor"),
        P("tm", "tensor"),
        P("tensor"),
        P("tensor"),
        P("tensor"),
    )
    return jax.shard_map(
        shards, mesh=mesh, in_specs=placed, out_specs=P("tm", "tensor"), check_vma=False
    )
```

```python
import functools
import math
import types

import jax
import jax.numpy as jnp
import numpy as np
from jax import lax
from jax.experimental import pallas as pl
from jax.experimental.pallas import tpu as pltpu
from jax.sharding import PartitionSpec as P

B16 = jnp.bfloat16
F32 = jnp.float32
MESH = pl.DeviceIdType.MESH

ENC_HD = 64
FRAMES = 1500
POOL = 4
LLM_HD = 128
PAD = 1536
ROWS = 384
TILES = PAD // ROWS
PROWS = ROWS // POOL
PART = PAD // 2
POOLED = PAD // POOL
SLOT = 8
FEAT = 320
WIDE = 384
LOG2E = math.log2(math.e)
NX = 4
NZ = 8
NC = 2
D_LLM = 3584
SEQ = 512
CHUNK = 56
PIECE = NC * CHUNK
BLOCK = 256
AROWS = 80
QKV = 1152


def dot(a, b):
    return jnp.dot(a, b, preferred_element_type=F32)


INPUTS = ("frames", "wq", "wk", "wv", "adapter", "wo", "text", "rope")
SMALL = ("gain", "owners", "counts", "llm_gain", "pq", "pk", "pv", "bq", "bk", "bv")
HBM, SEND, RECV = "hbm_", "_send", "_recv"
GROUPS = 4


def block_kernel(n_tm, n_t, names, *refs):
    r = types.SimpleNamespace(**dict(zip(names, refs, strict=True)))
    me = lax.axis_index("tm")
    t = lax.axis_index("tensor")
    z = me // (NX * NC)
    xx = lax.rem(me // NC, NX)
    c = lax.rem(me, NC)
    lane = lax.broadcasted_iota(jnp.int32, (1, 256), 1) // ENC_HD
    heads = 256 // ENC_HD

    def at(zz, xv, cv):
        return ((zz * NX + xv) * NC + cv, t)

    def x_other(k):
        return lax.rem(xx + k, NX)

    def t_other(k):
        return lax.rem(t + k, n_t)

    mate = at(z, xx, 1 - c)

    def remote(src, dst, send, recv, to):
        return pltpu.make_async_remote_copy(
            src_ref=src, dst_ref=dst, send_sem=send, recv_sem=recv, device_id=to, device_id_type=MESH
        )

    def drain(ref, sem):
        pltpu.make_async_copy(ref, ref, sem).wait()

    barrier = pltpu.get_barrier_semaphore()

    def greet(k, _):
        pl.semaphore_signal(
            barrier, inc=1, device_id=(lax.rem(me + k, n_tm), t), device_id_type=MESH
        )
        return 0

    lax.fori_loop(1, n_tm, greet, 0)
    for k in range(1, n_t):
        pl.semaphore_signal(barrier, inc=1, device_id=(me, t_other(k)), device_id_type=MESH)

    def fetched(name):
        return pltpu.make_async_copy(
            getattr(r, HBM + name), getattr(r, name), r.in_sem.at[INPUTS.index(name)]
        )

    for name in INPUTS:
        fetched(name).start()

    cut = 640

    def ring(k):
        return lax.rem(z + NZ + k, NZ)

    def ring_sent(buf, sems, k, to, step, cols=None):
        ref = buf.at[c, ring(k)]
        if cols is not None:
            ref = buf.at[c, ring(k), :, cols]
        remote(
            ref, ref, getattr(r, sems + SEND), getattr(r, sems + RECV).at[step], at(ring(to), xx, c)
        ).start()

    def to_mate(buf, sems, k):
        ref = buf.at[c, ring(k)]
        remote(ref, ref, getattr(r, sems + SEND), getattr(r, sems + RECV), mate).start()

    def ring_first(buf, sems):
        for k in (2, -2, 1, -1):
            ring_sent(buf, sems, 0, k, 0)

    def ring_second(buf, sems, mate_sems):
        drain(buf.at[c, pl.ds(0, 4)], getattr(r, sems + RECV).at[0])
        ring_sent(buf, sems, -2, 2, 1, slice(0, cut))
        ring_sent(buf, sems, 2, -2, 1, slice(cut, QKV))
        ring_sent(buf, sems, -2, 1, 1)
        ring_sent(buf, sems, 2, -1, 1)
        for k in (0, 1, -1, 2, -2):
            to_mate(buf, mate_sems, k)

    def ring_last(buf, sems, mate_sems):
        drain(buf.at[c, pl.ds(0, 3)], getattr(r, sems + RECV).at[1])
        for k in (3, -3, 4):
            to_mate(buf, mate_sems, k)

    def ring_done(buf, sems, mate_sems):
        drain(buf.at[c, pl.ds(0, NZ - 1)], getattr(r, sems + SEND))
        drain(buf.at[c], getattr(r, mate_sems + SEND))
        drain(buf.at[1 - c], getattr(r, mate_sems + RECV))

    nq, nk = r.pq.shape[1], r.pk.shape[1]
    own_w = r.wz.at[c, z]
    own_w[:, :nq] = r.pq[...]
    own_w[:, nq : nq + nk] = r.pk[...]
    own_w[:, nq + nk :] = r.pv[...]

    def adapter_rows(k):
        return remote(
            r.asel.at[xx],
            r.arow.at[t],
            r.as_send.at[k - 1],
            r.as_recv.at[k - 1],
            (me, t_other(k)),
        )

    def text_rows(k):
        xv = x_other(k)
        return remote(
            r.tp.at[xv],
            r.trow.at[xx],
            r.tp_send.at[k - 1],
            r.tp_recv.at[k - 1],
            at(z, xv, c),
        )

    for name in ("frames", "wq", "wk", "wv"):
        fetched(name).wait()
    tail_ref, frames_ref = r.tail, r.frames
    gain = r.gain[...].reshape(1, -1)
    tail_ref[...] = jnp.zeros_like(tail_ref)
    tail_ref[0 : FRAMES - 1280, :] = frames_ref[1280:FRAMES, :]
    prow = lax.broadcasted_iota(jnp.int32, (64, 256), 0)
    pcol = lax.broadcasted_iota(jnp.int32, (64, 256), 1)
    pool = jnp.where(pcol // POOL == prow, 0.25, 0.0).astype(B16)

    def project(raw, i):
        rows = pl.ds(pl.multiple_of(i * 256, 256), 256)
        x = raw.astype(F32)
        mean = jnp.mean(x, axis=-1, keepdims=True)
        cent = x - mean
        var = jnp.mean(cent * cent, axis=-1, keepdims=True)
        normed = (cent * lax.rsqrt(var + 1e-05) * gain).astype(B16)
        r.q[rows, :] = (dot(normed, r.wq[...]) * (ENC_HD**-0.5 * LOG2E)).astype(B16)
        r.kt[:, rows] = jnp.transpose(dot(normed, r.wk[...])).astype(B16)
        r.v[rows, :] = dot(normed, r.wv[...]).astype(B16)
        res = dot(pool, raw)
        prows = pl.ds(pl.multiple_of(i * 64, 64), 64)
        for tt in range(n_t):

            @pl.when(t == tt)
            def _():
                r.res[prows, :] = res[:, tt * FEAT : (tt + 1) * FEAT]

    def project_block(i, _):
        project(frames_ref[pl.ds(pl.multiple_of(i * 256, 256), 256), :], i)
        return 0

    lax.fori_loop(0, 2, project_block, 0)
    pl.semaphore_wait(barrier, n_tm - 1 + n_t - 1)
    ring_first(r.wz, "wz")
    lax.fori_loop(2, 5, project_block, 0)
    project(tail_ref[...], 5)

    onward = (lax.rem(me + 1, n_tm), t)

    def keys_on(part):
        cols = slice(part * PART, (part + 1) * PART)
        i = 2 * part
        return (
            remote(r.kt.at[:, cols], r.ktp.at[:, cols], r.kv_send.at[i], r.kv_recv.at[i], onward),
            remote(r.v.at[cols], r.vp.at[cols], r.kv_send.at[i + 1], r.kv_recv.at[i + 1], onward),
        )

    for part in range(2):
        for copy in keys_on(part):
            copy.start()

    fetched("adapter").wait()
    width = r.adapter.shape[1]
    llm_gain = r.llm_gain[...].reshape(1, -1)
    r.asel[...] = jnp.zeros_like(r.asel)
    r.gp[...] = jnp.zeros_like(r.gp)
    own_a = r.adapter[pl.ds(pl.multiple_of((c * NZ + z) * AROWS, AROWS), AROWS), :]
    for xv in range(NX):
        for zz in range(2):
            lo = zz * NX * PIECE + xv * PIECE
            r.asel[xv, :, zz * PIECE : (zz + 1) * PIECE] = own_a[:, lo : lo + PIECE]
            for tt in range(n_t):
                to = tt * BLOCK + zz * PIECE
                r.gp[xv, 0:1, to : to + PIECE] = llm_gain[:, tt * width + lo : tt * width + lo + PIECE]
    r.arow[t] = r.asel[xx]
    for k in range(1, n_t):
        adapter_rows(k).start()

    tail_lane = lax.broadcasted_iota(jnp.int32, (1, 128), 1) < FRAMES - (PAD - 128)

    def head_masks(values_ref, lo, size):
        for h in range(heads):
            r.vm[h, lo : lo + size] = jnp.where(
                lane == h, values_ref[lo : lo + size, :], jnp.ones((), B16)
            )

    def attend(rows, keys_ref, lo, size):
        q = r.q[rows, :]
        out = jnp.zeros((ROWS, 256), F32)
        top = jnp.zeros((ROWS, 256), F32)
        den = jnp.zeros((ROWS, 256), F32)
        for h in range(heads):
            s = dot(jnp.where(lane == h, q, jnp.zeros_like(q)), keys_ref[:, lo : lo + size])
            if lo + size == PAD:
                end = jnp.where(tail_lane, s[:, size - 128 :], -1e30)
                s = jnp.concatenate([s[:, : size - 128], end], axis=1)
            m = jnp.max(s, axis=1, keepdims=True)
            p = jnp.exp2(s - m).astype(B16)
            o = dot(p, r.vm[h, lo : lo + size])
            col = 255 if h < heads - 1 else 0
            out = jnp.where(lane == h, o, out)
            top = jnp.where(lane == h, m, top)
            den = jnp.where(lane == h, o[:, col : col + 1], den)
        return out, top, den

    head_masks(r.v, 0, PAD)

    def own_half(i, _):
        @pl.when(i == 2)
        def _():
            ring_second(r.wz, "wz", "wm")

        rows = pl.ds(pl.multiple_of(i * ROWS, ROWS), ROWS)
        out, top, den = attend(rows, r.kt, 0, PAD)
        r.o1[rows, :] = out
        r.m1[rows, :] = top
        r.l1[rows, :] = den
        return 0

    lax.fori_loop(0, TILES, own_half, 0)

    fetched("text").wait()
    text = r.text[...].astype(F32)
    power = jnp.mean(text * text, axis=-1, keepdims=True)
    text = (text * lax.rsqrt(power + 1e-06) * llm_gain).astype(B16)
    r.tp[...] = jnp.zeros_like(r.tp)
    for xv in range(NX):
        for tt in range(n_t):
            for zz in range(2):
                lo = tt * width + zz * NX * PIECE + xv * PIECE
                to = tt * BLOCK + zz * PIECE
                r.tp[xv, :, to : to + PIECE] = text[:, lo : lo + PIECE]
    r.trow[xx] = r.tp[xx]
    ring_last(r.wz, "wz", "wm")
    def fused_sent(k):
        return remote(
            r.fx.at[xx],
            r.fx.at[xx],
            r.fx_send.at[k - 1],
            r.fx_recv.at[k - 1],
            at(z, x_other(k), c),
        )

    def text_sent(k):
        xv = x_other(k)
        return remote(
            r.tsend.at[xv],
            r.trecv.at[xx],
            r.tx_send.at[k - 1],
            r.tx_recv.at[k - 1],
            at(z, xv, c),
        )

    def multiply_slab():
        ring_done(r.wz, "wz", "wm")
        for k in range(1, n_t):
            adapter_rows(k).wait()
        for tt in range(n_t):
            rows = [
                r.wz[cv, 2 * tt + zz].astype(F32) for zz in range(2) for cv in range(NC)
            ]
            rows.append(jnp.zeros((BLOCK - 2 * PIECE, QKV), F32))
            r.wslab[tt * BLOCK : (tt + 1) * BLOCK, :] = jnp.concatenate(rows, axis=0).astype(B16)
        fused = jnp.zeros((AROWS, QKV), F32)
        gains = r.gp[xx]
        for tt in range(n_t):
            cols = slice(tt * BLOCK, (tt + 1) * BLOCK)
            scaled = (r.arow[tt].astype(F32) * gains[0:1, cols]).astype(B16)
            fused = fused + dot(scaled, r.wslab[cols, :])
        r.fx[xx] = fused.astype(B16)
        for k in range(1, NX):
            fused_sent(k).start()

    def multiply_text():
        for k in range(1, NX):
            text_rows(k).wait()
        for xv in range(NX):
            r.tsend[xv] = dot(r.trow[xv], r.wslab[...]).astype(B16)
        r.trecv[xx] = r.tsend[xx]
        for k in range(1, NX):
            text_sent(k).start()

    def spread_fused():
        for k in range(1, NX):
            fused_sent(k).wait()
        total = r.fx[0].astype(F32)
        for xv in range(1, NX):
            total = total + r.fx[xv].astype(F32)
        r.fall[c, z] = total.astype(B16)
        ring_first(r.fall, "fz")
        for k in range(1, NX):
            text_rows(k).start()

    for copy in keys_on(0):
        copy.wait()
    head_masks(r.vp, 0, PART)
    fetched("wo").wait()
    begin = jnp.int32(0)
    openings = jnp.int32(0)
    for i in range(r.counts.shape[0]):
        openings = openings + jnp.where(begin == me, 1, 0)
        begin = begin + r.counts[i]
    is_open = openings > 0
    trow = lax.broadcasted_iota(jnp.int32, (PROWS, ROWS), 0)
    tcol = lax.broadcasted_iota(jnp.int32, (PROWS, ROWS), 1)
    tile_pool = jnp.where(tcol // POOL == trow, 0.25, 0.0).astype(B16)

    def summed(i, k):
        rows = pl.ds(pl.multiple_of(i * PROWS, PROWS), PROWS)
        to = t_other(k)
        return remote(
            r.part.at[to, rows],
            r.rs.at[t, rows],
            r.rs_send.at[i, k - 1],
            r.rs_recv.at[i, k - 1],
            (me, to),
        )

    def merged(rows, lo, size):
        out, top, den = attend(rows, r.ktp, lo, size)
        m1 = r.m1[rows, :]
        both = jnp.where(is_open, m1, jnp.maximum(m1, top))
        w1 = jnp.exp2(m1 - both)
        w2 = jnp.where(is_open, 0.0, jnp.exp2(jnp.minimum(top - both, 0.0)))
        return w1 * r.o1[rows, :] + w2 * out, both, w1 * r.l1[rows, :] + w2 * den

    def prior_first(i, _):
        rows = pl.ds(pl.multiple_of(i * ROWS, ROWS), ROWS)
        out, top, den = merged(rows, 0, PART)
        r.o1[rows, :] = out
        r.m1[rows, :] = top
        r.l1[rows, :] = den
        return 0

    lax.fori_loop(0, TILES // 2, prior_first, 0)
    multiply_slab()

    for copy in keys_on(1):
        copy.wait()
    head_masks(r.vp, PART, PART)

    def send_pooled(i, out, den):
        ctx = (out / den).astype(B16)
        pooled = dot(tile_pool, ctx).astype(B16)
        partial = dot(pooled, r.wo[...]).astype(B16)
        prows = pl.ds(pl.multiple_of(i * PROWS, PROWS), PROWS)
        for tt in range(n_t):
            r.part[tt, prows, :] = partial[:, tt * FEAT : (tt + 1) * FEAT]
        for k in range(1, n_t):
            summed(i, k).start()

    def prior_second(i, _):
        rows = pl.ds(pl.multiple_of(i * ROWS, ROWS), ROWS)
        out, _, den = merged(rows, PART, PART)
        send_pooled(i, out, den)
        return 0

    def prior_whole(i, _):
        @pl.when(i == TILES - 1)
        def _():
            spread_fused()

        rows = pl.ds(pl.multiple_of(i * ROWS, ROWS), ROWS)
        out, _, den = merged(rows, 0, PAD)
        send_pooled(i, out, den)
        return 0

    lax.fori_loop(0, TILES // 2, prior_second, 0)
    lax.fori_loop(TILES // 2, TILES, prior_whole, 0)

    owners = jnp.broadcast_to(r.owners[...].astype(F32), (128, POOLED))
    same = jnp.transpose(owners)[:, 0:1] == owners[0:1, :]
    first = lax.broadcasted_iota(jnp.int32, (POOLED, POOLED), 0)
    then = lax.broadcasted_iota(jnp.int32, (POOLED, POOLED), 1)
    ordinal = jnp.sum(jnp.where(same & (first < then), 1.0, 0.0), axis=0, keepdims=True)
    target = owners[0:1, :] * SLOT + ordinal
    slot_row = lax.broadcasted_iota(jnp.int32, (n_tm * SLOT, POOLED), 0)
    place = jnp.where(slot_row.astype(F32) == target, 1.0, 0.0).astype(B16)

    def summed_wait(i, _):
        for k in range(1, n_t):
            summed(i, k).wait()
        return 0

    lax.fori_loop(0, TILES, summed_wait, 0)

    total = r.part[t].astype(F32)
    for k in range(1, n_t):
        total = total + r.rs[t_other(k)].astype(F32)
    pooled = (r.res[...] + total).astype(B16)
    wide = jnp.concatenate([pooled, jnp.ones((POOLED, WIDE - FEAT), B16)], axis=1)
    slots_ref, x_ref = r.slots, r.x
    slots_ref[...] = dot(place, wide).reshape(n_tm, SLOT, WIDE).astype(B16)
    x_ref[t, 0] = slots_ref[me]
    members = n_tm // GROUPS

    for g in range(GROUPS):

        def routed_start(k, _, g=g):
            to = lax.rem(me + k, n_tm)
            remote(
                slots_ref.at[to], x_ref.at[t, k], r.a2a_send, r.a2a_recv.at[g], (to, t)
            ).start()
            return 0

        lax.fori_loop(max(1, g * members), (g + 1) * members, routed_start, 0)

    multiply_text()
    ring_second(r.fall, "fz", "fm")

    def handed(g, k):
        rows = pl.ds(g * members, members)
        ref = x_ref.at[t, rows]
        i = (k + 1) // 2
        return remote(
            ref, ref, r.ag_send.at[g, i], r.ag_recv.at[g, i], (me, lax.rem(t + n_t + k, n_t))
        )

    def relayed(g, k):
        part = members // 2
        rows = pl.ds(g * members + (0 if k > 0 else part), part)
        ref = x_ref.at[lax.rem(t + n_t - k, n_t), rows]
        i = (k + 1) // 2
        return remote(
            ref, ref, r.ar_send.at[g, i], r.ar_recv.at[g, i], (me, lax.rem(t + n_t + k, n_t))
        )

    def relay(g):
        for k in (1, -1):
            handed(g, k).wait()
        for k in (1, -1):
            relayed(g, k).start()

    for g in range(GROUPS):
        start = max(1, g * members)
        drain(x_ref.at[t, pl.ds(start, (g + 1) * members - start)], r.a2a_recv.at[g])
        for k in (1, -1):
            handed(g, k).start()
        if g > 0:
            relay(g - 1)
    used = SLOT - 1
    audio = n_tm * used
    fetched("rope").wait()
    srow = lax.broadcasted_iota(jnp.int32, (audio, n_tm * SLOT), 0)
    scol = lax.broadcasted_iota(jnp.int32, (audio, n_tm * SLOT), 1)
    source = (me - (scol >> 3)) & (n_tm - 1)
    row_to = source * used + (scol & (SLOT - 1))
    compact = jnp.where((row_to == srow) & ((scol & (SLOT - 1)) < used), 1.0, 0.0).astype(B16)

    def flat(tt):
        return x_ref[tt].astype(F32).reshape(n_tm * SLOT, WIDE).astype(B16)

    flags = dot(compact, flat(t))[:, FEAT : FEAT + 1]
    present = jnp.concatenate([flags, jnp.ones((SEQ - audio, 1), F32)], axis=0)
    present = jnp.broadcast_to(present, (SEQ, 128))
    row = lax.broadcasted_iota(jnp.int32, (SEQ, SEQ), 0)
    col = lax.broadcasted_iota(jnp.int32, (SEQ, SEQ), 1)
    until = jnp.where(col <= row, 1.0, 0.0).astype(B16)
    position = dot(until, present.astype(B16)) - 1.0
    chosen = jnp.where(col.astype(F32) == position[:, 0:1], 1.0, 0.0).astype(B16)
    high = r.rope[...].astype(B16)
    table = dot(chosen, high) + dot(chosen, (r.rope[...] - high.astype(F32)).astype(B16))
    cosine, sine = table[:, :LLM_HD], table[:, LLM_HD:]
    key_there = jnp.transpose(present)[0:1, :] > 0.5
    r.mask[...] = jnp.where(((col <= row) & key_there) | (col == row), 0.0, -1e30)

    relay(GROUPS - 1)
    drain(slots_ref.at[pl.ds(0, n_tm - 1)], r.a2a_send)
    for k in range(1, NX):
        text_sent(k).wait()
    for g in range(GROUPS):
        for k in (1, -1):
            relayed(g, k).wait()

    for tt in range(n_t):
        rows = dot(compact, flat(tt))
        r.xc[:, tt * FEAT : (tt + 1) * FEAT] = rows[:, :FEAT].astype(B16)

    adapted = dot(r.xc[...], r.adapter[...])
    power = jnp.sum(adapted * adapted, axis=1, keepdims=True)
    power = jnp.concatenate([power, jnp.zeros((SEQ - audio, 1), F32)], axis=0)
    power = jnp.transpose(jnp.broadcast_to(power, (SEQ, 128)))
    r.ss[t] = power[0:8, :]

    def power_sent(k):
        return remote(
            r.ss.at[t], r.ss.at[t], r.ss_send.at[k - 1], r.ss_recv.at[k - 1], (me, t_other(k))
        )

    for k in range(1, n_t):
        power_sent(k).start()

    ring_last(r.fall, "fz", "fm")
    ring_done(r.fall, "fz", "fm")
    r.qkv[0:audio, :] = dot(r.xc[...], r.fall[...].reshape(NC * NZ * AROWS, QKV))
    text_part = r.trecv[0].astype(F32)
    for xv in range(1, NX):
        text_part = text_part + r.trecv[xv].astype(F32)
    r.qkv[audio:SEQ, :] = text_part

    for k in range(1, n_t):
        power_sent(k).wait()
    power = r.ss[0]
    for tt in range(1, n_t):
        power = power + r.ss[tt]
    power = jnp.transpose(jnp.broadcast_to(power[0:1, :], (128, SEQ)))
    scale = lax.rsqrt(power * (1.0 / D_LLM) + 1e-06)
    row_of = lax.broadcasted_iota(jnp.int32, (SEQ, 128), 0)
    scale = jnp.where(row_of < audio, scale, 1.0)

    q_bias = r.bq[...].reshape(1, -1)

    def columns(i, bias):
        cols = slice(i * LLM_HD, (i + 1) * LLM_HD)
        return r.qkv[:, cols] * scale + bias

    def rotated(x):
        return x * cosine + pltpu.roll(x, LLM_HD // 2, 1) * sine

    q_heads = nq // LLM_HD
    keys = jnp.transpose(rotated(columns(q_heads, r.bk[...].reshape(1, -1)))).astype(B16)
    values = columns(q_heads + 1, r.bv[...].reshape(1, -1)).astype(B16)
    values = jnp.concatenate([values, jnp.ones((SEQ, LLM_HD), B16)], axis=1)
    for h in range(q_heads):
        bias = q_bias[:, h * LLM_HD : (h + 1) * LLM_HD]
        query = (rotated(columns(h, bias)) * (LLM_HD**-0.5 * LOG2E)).astype(B16)
        for lo in range(0, SEQ, 256):
            rows, end = slice(lo, lo + 256), lo + 256
            s = dot(query[rows], keys[:, :end]) + r.mask[rows, :end]
            m = jnp.max(s, axis=1, keepdims=True)
            o = dot(jnp.exp2(s - m).astype(B16), values[:end])
            ctx = o[:, :LLM_HD] / o[:, LLM_HD:] * present[rows]
            r.out[rows, h * LLM_HD : (h + 1) * LLM_HD] = ctx.astype(B16)


def rope_table():
    half = LLM_HD // 2
    freq = np.exp(
        np.arange(half, dtype=np.float32) * np.float32(-2.0 * math.log(1000000.0) / LLM_HD)
    ).astype(np.float32)
    angles = np.arange(SEQ, dtype=np.float32)[:, None] * freq[None, :]
    cosine = np.cos(angles.astype(np.float64)).astype(np.float32)
    sine = np.sin(angles.astype(np.float64)).astype(np.float32)
    return np.concatenate([cosine, cosine, -sine, sine], axis=1)


def run_block(n_tm, n_t, *args):
    vmem = pl.BlockSpec(memory_space=pltpu.VMEM)
    smem = pl.BlockSpec(memory_space=pltpu.SMEM)
    dma = pltpu.SemaphoreType.DMA
    audio = n_tm * (SLOT - 1)
    scratch = dict(
        tail=((256, 1280), B16),
        q=((PAD, 256), B16),
        kt=((256, PAD), B16),
        v=((PAD, 256), B16),
        ktp=((256, PAD), B16),
        vp=((PAD, 256), B16),
        vm=((256 // ENC_HD, PAD, 256), B16),
        o1=((PAD, 256), F32),
        m1=((PAD, 256), F32),
        l1=((PAD, 256), F32),
        res=((POOLED, FEAT), F32),
        part=((n_t, POOLED, FEAT), B16),
        rs=((n_t, POOLED, FEAT), B16),
        slots=((n_tm, SLOT, WIDE), B16),
        x=((n_t, n_tm, SLOT, WIDE), B16),
        wz=((NC, NZ, CHUNK, QKV), B16),
        wslab=((n_t * BLOCK, QKV), B16),
        tp=((NX, SEQ - audio, n_t * BLOCK), B16),
        gp=((NX, 8, n_t * BLOCK), F32),
        asel=((NX, AROWS, BLOCK), B16),
        arow=((n_t, AROWS, BLOCK), B16),
        trow=((NX, SEQ - audio, n_t * BLOCK), B16),
        tsend=((NX, SEQ - audio, QKV), B16),
        trecv=((NX, SEQ - audio, QKV), B16),
        fx=((NX, AROWS, QKV), B16),
        fall=((NC, NZ, AROWS, QKV), B16),
        xc=((audio, n_t * FEAT), B16),
        ss=((n_t, 8, SEQ), F32),
        qkv=((SEQ, QKV), F32),
        mask=((SEQ, SEQ), F32),
    )
    sems = dict(
        in_sem=(len(INPUTS),),
        kv_send=(4,),
        kv_recv=(4,),
        rs_send=(TILES, n_t - 1),
        rs_recv=(TILES, n_t - 1),
        a2a_send=(),
        a2a_recv=(GROUPS,),
        ag_send=(GROUPS, 2),
        ag_recv=(GROUPS, 2),
        ar_send=(GROUPS, 2),
        ar_recv=(GROUPS, 2),
        wz_send=(),
        wz_recv=(2,),
        wm_send=(),
        wm_recv=(),
        as_send=(n_t - 1,),
        as_recv=(n_t - 1,),
        tp_send=(NX - 1,),
        tp_recv=(NX - 1,),
        fx_send=(NX - 1,),
        fx_recv=(NX - 1,),
        tx_send=(NX - 1,),
        tx_recv=(NX - 1,),
        fz_send=(),
        fz_recv=(2,),
        fm_send=(),
        fm_recv=(),
        ss_send=(n_t - 1,),
        ss_recv=(n_t - 1,),
    )
    held = {n: (a.shape, a.dtype) for n, a in zip(INPUTS, args, strict=False)} | scratch
    shapes = [pltpu.VMEM(*a) for a in held.values()]
    shapes += [dma(a) if a else dma for a in sems.values()]
    names = [HBM + n for n in INPUTS] + [*SMALL, "out", *held, *sems]
    return pl.pallas_call(
        functools.partial(block_kernel, n_tm, n_t, names),
        out_shape=jax.ShapeDtypeStruct((SEQ, args[len(INPUTS) + SMALL.index("pq")].shape[1]), B16),
        in_specs=[pl.BlockSpec(memory_space=pl.ANY)] * len(INPUTS)
        + [smem if n == "counts" else vmem for n in SMALL],
        out_specs=vmem,
        scratch_shapes=shapes,
        compiler_params=pltpu.CompilerParams(
            collective_id=0, has_side_effects=True, vmem_limit_bytes=62 << 20
        ),
        cost_estimate=pl.CostEstimate(
            flops=20_000_000_000, bytes_accessed=20_000_000, transcendentals=20_000_000
        ),
    )(*args)


def shards(
    enc_frames,
    span_counts,
    enc_gain,
    enc_wq,
    enc_wk,
    enc_wv,
    enc_wo,
    adapter,
    owner_map,
    text_embeds,
    llm_gain,
    llm_wq,
    llm_wk,
    llm_wv,
    llm_bq,
    llm_bk,
    llm_bv,
):
    n_tm = lax.axis_size("tm")
    n_t = lax.axis_size("tensor")
    me = lax.axis_index("tm")
    count = FRAMES // POOL
    owners = lax.dynamic_slice_in_dim(owner_map, me * count, count, 0)[:, 0]
    owners = jnp.pad(owners, (0, POOLED - count), constant_values=-n_tm)[None, :]
    return run_block(
        n_tm,
        n_t,
        enc_frames,
        enc_wq,
        enc_wk,
        enc_wv,
        adapter,
        enc_wo,
        text_embeds,
        jnp.asarray(rope_table()),
        enc_gain,
        owners,
        span_counts,
        llm_gain,
        llm_wq,
        llm_wk,
        llm_wv,
        llm_bq,
        llm_bk,
        llm_bv,
    )


def solution(mesh):
    placed = (
        P("tm", None),
        P(),
        P(),
        P(None, "tensor"),
        P(None, "tensor"),
        P(None, "tensor"),
        P("tensor", None),
        P(None, "tensor"),
        P(),
        P("tm", None),
        P(),
        P("tm", "tensor"),
        P("tm", "tensor"),
        P("tm", "tensor"),
        P("tensor"),
        P("tensor"),
        P("tensor"),
    )
    return jax.shard_map(
        shards, mesh=mesh, in_specs=placed, out_specs=P("tm", "tensor"), check_vma=False
    )
```

```python
import functools
import math
import types

import jax
import jax.numpy as jnp
import numpy as np
from jax import lax
from jax.experimental import pallas as pl
from jax.experimental.pallas import tpu as pltpu
from jax.sharding import PartitionSpec as P

B16 = jnp.bfloat16
F32 = jnp.float32
MESH = pl.DeviceIdType.MESH

ENC_HD = 64
FRAMES = 1500
POOL = 4
LLM_HD = 128
PAD = 1536
ROWS = 384
TILES = PAD // ROWS
PROWS = ROWS // POOL
PART = PAD // 2
POOLED = PAD // POOL
SLOT = 8
FEAT = 320
WIDE = 384
LOG2E = math.log2(math.e)
NX = 4
NZ = 8
NC = 2
D_LLM = 3584
SEQ = 512
CHUNK = 56
PIECE = NC * CHUNK
BLOCK = 256
AROWS = 80
QKV = 1152


def dot(a, b):
    return jnp.dot(a, b, preferred_element_type=F32)


INPUTS = ("frames", "wq", "wk", "wv", "adapter", "wo", "text", "rope")
SMALL = ("gain", "owners", "counts", "llm_gain", "pq", "pk", "pv", "bq", "bk", "bv")
HBM, SEND, RECV = "hbm_", "_send", "_recv"
GROUPS = 4


def block_kernel(n_tm, n_t, names, *refs):
    r = types.SimpleNamespace(**dict(zip(names, refs, strict=True)))
    me = lax.axis_index("tm")
    t = lax.axis_index("tensor")
    z = me // (NX * NC)
    xx = lax.rem(me // NC, NX)
    c = lax.rem(me, NC)
    lane = lax.broadcasted_iota(jnp.int32, (1, 256), 1) // ENC_HD
    heads = 256 // ENC_HD

    def at(zz, xv, cv):
        return ((zz * NX + xv) * NC + cv, t)

    def x_other(k):
        return lax.rem(xx + k, NX)

    def t_other(k):
        return lax.rem(t + k, n_t)

    mate = at(z, xx, 1 - c)

    def remote(src, dst, send, recv, to):
        return pltpu.make_async_remote_copy(
            src_ref=src, dst_ref=dst, send_sem=send, recv_sem=recv, device_id=to, device_id_type=MESH
        )

    def drain(ref, sem):
        pltpu.make_async_copy(ref, ref, sem).wait()

    barrier = pltpu.get_barrier_semaphore()

    def greet(k, _):
        pl.semaphore_signal(
            barrier, inc=1, device_id=(lax.rem(me + k, n_tm), t), device_id_type=MESH
        )
        return 0

    lax.fori_loop(1, n_tm, greet, 0)
    for k in range(1, n_t):
        pl.semaphore_signal(barrier, inc=1, device_id=(me, t_other(k)), device_id_type=MESH)

    def fetched(name):
        return pltpu.make_async_copy(
            getattr(r, HBM + name), getattr(r, name), r.in_sem.at[INPUTS.index(name)]
        )

    for name in INPUTS:
        fetched(name).start()

    cut = 640

    def ring(k):
        return lax.rem(z + NZ + k, NZ)

    def ring_sent(buf, sems, k, to, step, cols=None):
        ref = buf.at[c, ring(k)]
        if cols is not None:
            ref = buf.at[c, ring(k), :, cols]
        remote(
            ref, ref, getattr(r, sems + SEND), getattr(r, sems + RECV).at[step], at(ring(to), xx, c)
        ).start()

    def to_mate(buf, sems, k):
        ref = buf.at[c, ring(k)]
        remote(ref, ref, getattr(r, sems + SEND), getattr(r, sems + RECV), mate).start()

    def ring_first(buf, sems):
        for k in (2, -2, 1, -1):
            ring_sent(buf, sems, 0, k, 0)

    def ring_second(buf, sems, mate_sems):
        drain(buf.at[c, pl.ds(0, 4)], getattr(r, sems + RECV).at[0])
        ring_sent(buf, sems, -2, 2, 1, slice(0, cut))
        ring_sent(buf, sems, 2, -2, 1, slice(cut, QKV))
        ring_sent(buf, sems, -2, 1, 1)
        ring_sent(buf, sems, 2, -1, 1)
        for k in (0, 1, -1, 2, -2):
            to_mate(buf, mate_sems, k)

    def ring_last(buf, sems, mate_sems):
        drain(buf.at[c, pl.ds(0, 3)], getattr(r, sems + RECV).at[1])
        for k in (3, -3, 4):
            to_mate(buf, mate_sems, k)

    def ring_done(buf, sems, mate_sems):
        drain(buf.at[c, pl.ds(0, NZ - 1)], getattr(r, sems + SEND))
        drain(buf.at[c], getattr(r, mate_sems + SEND))
        drain(buf.at[1 - c], getattr(r, mate_sems + RECV))

    nq, nk = r.pq.shape[1], r.pk.shape[1]
    own_w = r.wz.at[c, z]
    own_w[:, :nq] = r.pq[...]
    own_w[:, nq : nq + nk] = r.pk[...]
    own_w[:, nq + nk :] = r.pv[...]

    def adapter_rows(k):
        return remote(
            r.asel.at[xx],
            r.arow.at[t],
            r.as_send.at[k - 1],
            r.as_recv.at[k - 1],
            (me, t_other(k)),
        )

    def text_rows(k):
        xv = x_other(k)
        return remote(
            r.tp.at[xv],
            r.trow.at[xx],
            r.tp_send.at[k - 1],
            r.tp_recv.at[k - 1],
            at(z, xv, c),
        )

    for name in ("frames", "wq", "wk", "wv"):
        fetched(name).wait()
    tail_ref, frames_ref = r.tail, r.frames
    gain = r.gain[...].reshape(1, -1)
    tail_ref[...] = jnp.zeros_like(tail_ref)
    tail_ref[0 : FRAMES - 1280, :] = frames_ref[1280:FRAMES, :]
    prow = lax.broadcasted_iota(jnp.int32, (64, 256), 0)
    pcol = lax.broadcasted_iota(jnp.int32, (64, 256), 1)
    pool = jnp.where(pcol // POOL == prow, 0.25, 0.0).astype(B16)

    def project(raw, i):
        rows = pl.ds(pl.multiple_of(i * 256, 256), 256)
        x = raw.astype(F32)
        mean = jnp.mean(x, axis=-1, keepdims=True)
        cent = x - mean
        var = jnp.mean(cent * cent, axis=-1, keepdims=True)
        normed = (cent * lax.rsqrt(var + 1e-05) * gain).astype(B16)
        r.q[rows, :] = (dot(normed, r.wq[...]) * (ENC_HD**-0.5 * LOG2E)).astype(B16)
        r.kt[:, rows] = jnp.transpose(dot(normed, r.wk[...])).astype(B16)
        r.v[rows, :] = dot(normed, r.wv[...]).astype(B16)
        res = dot(pool, raw)
        prows = pl.ds(pl.multiple_of(i * 64, 64), 64)
        for tt in range(n_t):

            @pl.when(t == tt)
            def _():
                r.res[prows, :] = res[:, tt * FEAT : (tt + 1) * FEAT]

    def project_block(i, _):
        project(frames_ref[pl.ds(pl.multiple_of(i * 256, 256), 256), :], i)
        return 0

    lax.fori_loop(0, 2, project_block, 0)
    pl.semaphore_wait(barrier, n_tm - 1 + n_t - 1)
    ring_first(r.wz, "wz")
    lax.fori_loop(2, 5, project_block, 0)
    project(tail_ref[...], 5)

    onward = (lax.rem(me + 1, n_tm), t)

    def keys_on(part):
        cols = slice(part * PART, (part + 1) * PART)
        i = 2 * part
        return (
            remote(r.kt.at[:, cols], r.ktp.at[:, cols], r.kv_send.at[i], r.kv_recv.at[i], onward),
            remote(r.v.at[cols], r.vp.at[cols], r.kv_send.at[i + 1], r.kv_recv.at[i + 1], onward),
        )

    for part in range(2):
        for copy in keys_on(part):
            copy.start()

    fetched("adapter").wait()
    width = r.adapter.shape[1]
    llm_gain = r.llm_gain[...].reshape(1, -1)
    r.asel[...] = jnp.zeros_like(r.asel)
    r.gp[...] = jnp.zeros_like(r.gp)
    own_a = r.adapter[pl.ds(pl.multiple_of((c * NZ + z) * AROWS, AROWS), AROWS), :]
    for xv in range(NX):
        for zz in range(2):
            lo = zz * NX * PIECE + xv * PIECE
            r.asel[xv, :, zz * PIECE : (zz + 1) * PIECE] = own_a[:, lo : lo + PIECE]
            for tt in range(n_t):
                to = tt * BLOCK + zz * PIECE
                r.gp[xv, 0:1, to : to + PIECE] = llm_gain[:, tt * width + lo : tt * width + lo + PIECE]
    r.arow[t] = r.asel[xx]
    for k in range(1, n_t):
        adapter_rows(k).start()

    tail_lane = lax.broadcasted_iota(jnp.int32, (1, 128), 1) < FRAMES - (PAD - 128)

    def head_masks(values_ref, lo, size):
        for h in range(heads):
            r.vm[h, lo : lo + size] = jnp.where(
                lane == h, values_ref[lo : lo + size, :], jnp.ones((), B16)
            )

    def attend(rows, keys_ref, lo, size):
        q = r.q[rows, :]
        out = jnp.zeros((ROWS, 256), F32)
        top = jnp.zeros((ROWS, 256), F32)
        den = jnp.zeros((ROWS, 256), F32)
        for h in range(heads):
            s = dot(jnp.where(lane == h, q, jnp.zeros_like(q)), keys_ref[:, lo : lo + size])
            if lo + size == PAD:
                end = jnp.where(tail_lane, s[:, size - 128 :], -1e30)
                s = jnp.concatenate([s[:, : size - 128], end], axis=1)
            m = jnp.max(s, axis=1, keepdims=True)
            p = jnp.exp2(s - m).astype(B16)
            o = dot(p, r.vm[h, lo : lo + size])
            col = 255 if h < heads - 1 else 0
            out = jnp.where(lane == h, o, out)
            top = jnp.where(lane == h, m, top)
            den = jnp.where(lane == h, o[:, col : col + 1], den)
        return out, top, den

    head_masks(r.v, 0, PAD)

    def own_half(i, _):
        @pl.when(i == 2)
        def _():
            ring_second(r.wz, "wz", "wm")

        rows = pl.ds(pl.multiple_of(i * ROWS, ROWS), ROWS)
        out, top, den = attend(rows, r.kt, 0, PAD)
        r.o1[rows, :] = out
        r.m1[rows, :] = top
        r.l1[rows, :] = den
        return 0

    lax.fori_loop(0, TILES, own_half, 0)

    fetched("text").wait()
    text = r.text[...].astype(F32)
    power = jnp.mean(text * text, axis=-1, keepdims=True)
    text = (text * lax.rsqrt(power + 1e-06) * llm_gain).astype(B16)
    r.tp[...] = jnp.zeros_like(r.tp)
    for xv in range(NX):
        for tt in range(n_t):
            for zz in range(2):
                lo = tt * width + zz * NX * PIECE + xv * PIECE
                to = tt * BLOCK + zz * PIECE
                r.tp[xv, :, to : to + PIECE] = text[:, lo : lo + PIECE]
    r.trow[xx] = r.tp[xx]
    ring_last(r.wz, "wz", "wm")
    for k in range(1, NX):
        text_rows(k).start()
    def fused_sent(k):
        return remote(
            r.fx.at[xx],
            r.fx.at[xx],
            r.fx_send.at[k - 1],
            r.fx_recv.at[k - 1],
            at(z, x_other(k), c),
        )

    def text_sent(k):
        xv = x_other(k)
        return remote(
            r.tsend.at[xv],
            r.trecv.at[xx],
            r.tx_send.at[k - 1],
            r.tx_recv.at[k - 1],
            at(z, xv, c),
        )

    def multiply_slab():
        ring_done(r.wz, "wz", "wm")
        for k in range(1, n_t):
            adapter_rows(k).wait()
        for tt in range(n_t):
            rows = [
                r.wz[cv, 2 * tt + zz].astype(F32) for zz in range(2) for cv in range(NC)
            ]
            rows.append(jnp.zeros((BLOCK - 2 * PIECE, QKV), F32))
            r.wslab[tt * BLOCK : (tt + 1) * BLOCK, :] = jnp.concatenate(rows, axis=0).astype(B16)
        fused = jnp.zeros((AROWS, QKV), F32)
        gains = r.gp[xx]
        for tt in range(n_t):
            cols = slice(tt * BLOCK, (tt + 1) * BLOCK)
            scaled = (r.arow[tt].astype(F32) * gains[0:1, cols]).astype(B16)
            fused = fused + dot(scaled, r.wslab[cols, :])
        r.fx[xx] = fused.astype(B16)
        for k in range(1, NX):
            fused_sent(k).start()

    def multiply_text():
        for k in range(1, NX):
            text_rows(k).wait()
        for xv in range(NX):
            r.tsend[xv] = dot(r.trow[xv], r.wslab[...]).astype(B16)
        r.trecv[xx] = r.tsend[xx]
        for k in range(1, NX):
            text_sent(k).start()

    def spread_fused():
        for k in range(1, NX):
            fused_sent(k).wait()
        total = r.fx[0].astype(F32)
        for xv in range(1, NX):
            total = total + r.fx[xv].astype(F32)
        r.fall[c, z] = total.astype(B16)
        ring_first(r.fall, "fz")

    for copy in keys_on(0):
        copy.wait()
    head_masks(r.vp, 0, PART)
    fetched("wo").wait()
    begin = jnp.int32(0)
    openings = jnp.int32(0)
    for i in range(r.counts.shape[0]):
        openings = openings + jnp.where(begin == me, 1, 0)
        begin = begin + r.counts[i]
    is_open = openings > 0
    trow = lax.broadcasted_iota(jnp.int32, (PROWS, ROWS), 0)
    tcol = lax.broadcasted_iota(jnp.int32, (PROWS, ROWS), 1)
    tile_pool = jnp.where(tcol // POOL == trow, 0.25, 0.0).astype(B16)

    def summed(i, k):
        rows = pl.ds(pl.multiple_of(i * PROWS, PROWS), PROWS)
        to = t_other(k)
        return remote(
            r.part.at[to, rows],
            r.rs.at[t, rows],
            r.rs_send.at[i, k - 1],
            r.rs_recv.at[i, k - 1],
            (me, to),
        )

    def merged(rows, lo, size):
        out, top, den = attend(rows, r.ktp, lo, size)
        m1 = r.m1[rows, :]
        both = jnp.where(is_open, m1, jnp.maximum(m1, top))
        w1 = jnp.exp2(m1 - both)
        w2 = jnp.where(is_open, 0.0, jnp.exp2(jnp.minimum(top - both, 0.0)))
        return w1 * r.o1[rows, :] + w2 * out, both, w1 * r.l1[rows, :] + w2 * den

    def prior_first(i, _):
        rows = pl.ds(pl.multiple_of(i * ROWS, ROWS), ROWS)
        out, top, den = merged(rows, 0, PART)
        r.o1[rows, :] = out
        r.m1[rows, :] = top
        r.l1[rows, :] = den
        return 0

    lax.fori_loop(0, TILES // 2, prior_first, 0)
    multiply_slab()

    for copy in keys_on(1):
        copy.wait()
    head_masks(r.vp, PART, PART)

    def send_pooled(i, out, den):
        ctx = (out / den).astype(B16)
        pooled = dot(tile_pool, ctx).astype(B16)
        partial = dot(pooled, r.wo[...]).astype(B16)
        prows = pl.ds(pl.multiple_of(i * PROWS, PROWS), PROWS)
        for tt in range(n_t):
            r.part[tt, prows, :] = partial[:, tt * FEAT : (tt + 1) * FEAT]
        for k in range(1, n_t):
            summed(i, k).start()

    def prior_second(i, _):
        rows = pl.ds(pl.multiple_of(i * ROWS, ROWS), ROWS)
        out, _, den = merged(rows, PART, PART)
        send_pooled(i, out, den)
        return 0

    def prior_whole(i, _):
        @pl.when(i == TILES - 1)
        def _():
            spread_fused()

        rows = pl.ds(pl.multiple_of(i * ROWS, ROWS), ROWS)
        out, _, den = merged(rows, 0, PAD)
        send_pooled(i, out, den)
        return 0

    lax.fori_loop(0, TILES // 2, prior_second, 0)
    lax.fori_loop(TILES // 2, TILES, prior_whole, 0)

    owners = jnp.broadcast_to(r.owners[...].astype(F32), (128, POOLED))
    same = jnp.transpose(owners)[:, 0:1] == owners[0:1, :]
    first = lax.broadcasted_iota(jnp.int32, (POOLED, POOLED), 0)
    then = lax.broadcasted_iota(jnp.int32, (POOLED, POOLED), 1)
    ordinal = jnp.sum(jnp.where(same & (first < then), 1.0, 0.0), axis=0, keepdims=True)
    target = owners[0:1, :] * SLOT + ordinal
    slot_row = lax.broadcasted_iota(jnp.int32, (n_tm * SLOT, POOLED), 0)
    place = jnp.where(slot_row.astype(F32) == target, 1.0, 0.0).astype(B16)

    multiply_text()

    def summed_wait(i, _):
        for k in range(1, n_t):
            summed(i, k).wait()
        return 0

    lax.fori_loop(0, TILES, summed_wait, 0)

    total = r.part[t].astype(F32)
    for k in range(1, n_t):
        total = total + r.rs[t_other(k)].astype(F32)
    pooled = (r.res[...] + total).astype(B16)
    wide = jnp.concatenate([pooled, jnp.ones((POOLED, WIDE - FEAT), B16)], axis=1)
    slots_ref, x_ref = r.slots, r.x
    slots_ref[...] = dot(place, wide).reshape(n_tm, SLOT, WIDE).astype(B16)
    x_ref[t, 0] = slots_ref[me]
    members = n_tm // GROUPS

    for g in range(GROUPS):

        def routed_start(k, _, g=g):
            to = lax.rem(me + k, n_tm)
            remote(
                slots_ref.at[to], x_ref.at[t, k], r.a2a_send, r.a2a_recv.at[g], (to, t)
            ).start()
            return 0

        lax.fori_loop(max(1, g * members), (g + 1) * members, routed_start, 0)

    def handed(g, k):
        rows = pl.ds(g * members, members)
        ref = x_ref.at[t, rows]
        i = (k + 1) // 2
        return remote(
            ref, ref, r.ag_send.at[g, i], r.ag_recv.at[g, i], (me, lax.rem(t + n_t + k, n_t))
        )

    def relayed(g, k):
        part = members // 2
        rows = pl.ds(g * members + (0 if k > 0 else part), part)
        ref = x_ref.at[lax.rem(t + n_t - k, n_t), rows]
        i = (k + 1) // 2
        return remote(
            ref, ref, r.ar_send.at[g, i], r.ar_recv.at[g, i], (me, lax.rem(t + n_t + k, n_t))
        )

    def relay(g):
        for k in (1, -1):
            handed(g, k).wait()
        for k in (1, -1):
            relayed(g, k).start()

    for g in range(GROUPS):
        start = max(1, g * members)
        drain(x_ref.at[t, pl.ds(start, (g + 1) * members - start)], r.a2a_recv.at[g])
        for k in (1, -1):
            handed(g, k).start()
        if g == GROUPS - 1:
            ring_second(r.fall, "fz", "fm")
        if g > 0:
            relay(g - 1)
    used = SLOT - 1
    audio = n_tm * used
    fetched("rope").wait()
    srow = lax.broadcasted_iota(jnp.int32, (audio, n_tm * SLOT), 0)
    scol = lax.broadcasted_iota(jnp.int32, (audio, n_tm * SLOT), 1)
    source = (me - (scol >> 3)) & (n_tm - 1)
    row_to = source * used + (scol & (SLOT - 1))
    compact = jnp.where((row_to == srow) & ((scol & (SLOT - 1)) < used), 1.0, 0.0).astype(B16)

    def flat(tt):
        return x_ref[tt].astype(F32).reshape(n_tm * SLOT, WIDE).astype(B16)

    flags = dot(compact, flat(t))[:, FEAT : FEAT + 1]
    present = jnp.concatenate([flags, jnp.ones((SEQ - audio, 1), F32)], axis=0)
    present = jnp.broadcast_to(present, (SEQ, 128))
    row = lax.broadcasted_iota(jnp.int32, (SEQ, SEQ), 0)
    col = lax.broadcasted_iota(jnp.int32, (SEQ, SEQ), 1)
    until = jnp.where(col <= row, 1.0, 0.0).astype(B16)
    position = dot(until, present.astype(B16)) - 1.0
    chosen = jnp.where(col.astype(F32) == position[:, 0:1], 1.0, 0.0).astype(B16)
    high = r.rope[...].astype(B16)
    table = dot(chosen, high) + dot(chosen, (r.rope[...] - high.astype(F32)).astype(B16))
    cosine, sine = table[:, :LLM_HD], table[:, LLM_HD:]
    key_there = jnp.transpose(present)[0:1, :] > 0.5
    r.mask[...] = jnp.where(((col <= row) & key_there) | (col == row), 0.0, -1e30)

    relay(GROUPS - 1)
    drain(slots_ref.at[pl.ds(0, n_tm - 1)], r.a2a_send)
    for k in range(1, NX):
        text_sent(k).wait()
    for g in range(GROUPS):
        for k in (1, -1):
            relayed(g, k).wait()

    for tt in range(n_t):
        rows = dot(compact, flat(tt))
        r.xc[:, tt * FEAT : (tt + 1) * FEAT] = rows[:, :FEAT].astype(B16)

    adapted = dot(r.xc[...], r.adapter[...])
    power = jnp.sum(adapted * adapted, axis=1, keepdims=True)
    power = jnp.concatenate([power, jnp.zeros((SEQ - audio, 1), F32)], axis=0)
    power = jnp.transpose(jnp.broadcast_to(power, (SEQ, 128)))
    r.ss[t] = power[0:8, :]

    def power_sent(k):
        return remote(
            r.ss.at[t], r.ss.at[t], r.ss_send.at[k - 1], r.ss_recv.at[k - 1], (me, t_other(k))
        )

    for k in range(1, n_t):
        power_sent(k).start()

    ring_last(r.fall, "fz", "fm")
    ring_done(r.fall, "fz", "fm")
    r.qkv[0:audio, :] = dot(r.xc[...], r.fall[...].reshape(NC * NZ * AROWS, QKV))
    text_part = r.trecv[0].astype(F32)
    for xv in range(1, NX):
        text_part = text_part + r.trecv[xv].astype(F32)
    r.qkv[audio:SEQ, :] = text_part

    for k in range(1, n_t):
        power_sent(k).wait()
    power = r.ss[0]
    for tt in range(1, n_t):
        power = power + r.ss[tt]
    power = jnp.transpose(jnp.broadcast_to(power[0:1, :], (128, SEQ)))
    scale = lax.rsqrt(power * (1.0 / D_LLM) + 1e-06)
    row_of = lax.broadcasted_iota(jnp.int32, (SEQ, 128), 0)
    scale = jnp.where(row_of < audio, scale, 1.0)

    q_bias = r.bq[...].reshape(1, -1)

    def columns(i, bias):
        cols = slice(i * LLM_HD, (i + 1) * LLM_HD)
        return r.qkv[:, cols] * scale + bias

    def rotated(x):
        return x * cosine + pltpu.roll(x, LLM_HD // 2, 1) * sine

    q_heads = nq // LLM_HD
    keys = jnp.transpose(rotated(columns(q_heads, r.bk[...].reshape(1, -1)))).astype(B16)
    values = columns(q_heads + 1, r.bv[...].reshape(1, -1)).astype(B16)
    values = jnp.concatenate([values, jnp.ones((SEQ, LLM_HD), B16)], axis=1)
    for h in range(q_heads):
        bias = q_bias[:, h * LLM_HD : (h + 1) * LLM_HD]
        query = (rotated(columns(h, bias)) * (LLM_HD**-0.5 * LOG2E)).astype(B16)
        for lo in range(0, SEQ, 256):
            rows, end = slice(lo, lo + 256), lo + 256
            s = dot(query[rows], keys[:, :end]) + r.mask[rows, :end]
            m = jnp.max(s, axis=1, keepdims=True)
            o = dot(jnp.exp2(s - m).astype(B16), values[:end])
            ctx = o[:, :LLM_HD] / o[:, LLM_HD:] * present[rows]
            r.out[rows, h * LLM_HD : (h + 1) * LLM_HD] = ctx.astype(B16)


def rope_table():
    half = LLM_HD // 2
    freq = np.exp(
        np.arange(half, dtype=np.float32) * np.float32(-2.0 * math.log(1000000.0) / LLM_HD)
    ).astype(np.float32)
    angles = np.arange(SEQ, dtype=np.float32)[:, None] * freq[None, :]
    cosine = np.cos(angles.astype(np.float64)).astype(np.float32)
    sine = np.sin(angles.astype(np.float64)).astype(np.float32)
    return np.concatenate([cosine, cosine, -sine, sine], axis=1)


def run_block(n_tm, n_t, *args):
    vmem = pl.BlockSpec(memory_space=pltpu.VMEM)
    smem = pl.BlockSpec(memory_space=pltpu.SMEM)
    dma = pltpu.SemaphoreType.DMA
    audio = n_tm * (SLOT - 1)
    scratch = dict(
        tail=((256, 1280), B16),
        q=((PAD, 256), B16),
        kt=((256, PAD), B16),
        v=((PAD, 256), B16),
        ktp=((256, PAD), B16),
        vp=((PAD, 256), B16),
        vm=((256 // ENC_HD, PAD, 256), B16),
        o1=((PAD, 256), F32),
        m1=((PAD, 256), F32),
        l1=((PAD, 256), F32),
        res=((POOLED, FEAT), F32),
        part=((n_t, POOLED, FEAT), B16),
        rs=((n_t, POOLED, FEAT), B16),
        slots=((n_tm, SLOT, WIDE), B16),
        x=((n_t, n_tm, SLOT, WIDE), B16),
        wz=((NC, NZ, CHUNK, QKV), B16),
        wslab=((n_t * BLOCK, QKV), B16),
        tp=((NX, SEQ - audio, n_t * BLOCK), B16),
        gp=((NX, 8, n_t * BLOCK), F32),
        asel=((NX, AROWS, BLOCK), B16),
        arow=((n_t, AROWS, BLOCK), B16),
        trow=((NX, SEQ - audio, n_t * BLOCK), B16),
        tsend=((NX, SEQ - audio, QKV), B16),
        trecv=((NX, SEQ - audio, QKV), B16),
        fx=((NX, AROWS, QKV), B16),
        fall=((NC, NZ, AROWS, QKV), B16),
        xc=((audio, n_t * FEAT), B16),
        ss=((n_t, 8, SEQ), F32),
        qkv=((SEQ, QKV), F32),
        mask=((SEQ, SEQ), F32),
    )
    sems = dict(
        in_sem=(len(INPUTS),),
        kv_send=(4,),
        kv_recv=(4,),
        rs_send=(TILES, n_t - 1),
        rs_recv=(TILES, n_t - 1),
        a2a_send=(),
        a2a_recv=(GROUPS,),
        ag_send=(GROUPS, 2),
        ag_recv=(GROUPS, 2),
        ar_send=(GROUPS, 2),
        ar_recv=(GROUPS, 2),
        wz_send=(),
        wz_recv=(2,),
        wm_send=(),
        wm_recv=(),
        as_send=(n_t - 1,),
        as_recv=(n_t - 1,),
        tp_send=(NX - 1,),
        tp_recv=(NX - 1,),
        fx_send=(NX - 1,),
        fx_recv=(NX - 1,),
        tx_send=(NX - 1,),
        tx_recv=(NX - 1,),
        fz_send=(),
        fz_recv=(2,),
        fm_send=(),
        fm_recv=(),
        ss_send=(n_t - 1,),
        ss_recv=(n_t - 1,),
    )
    held = {n: (a.shape, a.dtype) for n, a in zip(INPUTS, args, strict=False)} | scratch
    shapes = [pltpu.VMEM(*a) for a in held.values()]
    shapes += [dma(a) if a else dma for a in sems.values()]
    names = [HBM + n for n in INPUTS] + [*SMALL, "out", *held, *sems]
    return pl.pallas_call(
        functools.partial(block_kernel, n_tm, n_t, names),
        out_shape=jax.ShapeDtypeStruct((SEQ, args[len(INPUTS) + SMALL.index("pq")].shape[1]), B16),
        in_specs=[pl.BlockSpec(memory_space=pl.ANY)] * len(INPUTS)
        + [smem if n == "counts" else vmem for n in SMALL],
        out_specs=vmem,
        scratch_shapes=shapes,
        compiler_params=pltpu.CompilerParams(
            collective_id=0, has_side_effects=True, vmem_limit_bytes=62 << 20
        ),
        cost_estimate=pl.CostEstimate(
            flops=20_000_000_000, bytes_accessed=20_000_000, transcendentals=20_000_000
        ),
    )(*args)


def shards(
    enc_frames,
    span_counts,
    enc_gain,
    enc_wq,
    enc_wk,
    enc_wv,
    enc_wo,
    adapter,
    owner_map,
    text_embeds,
    llm_gain,
    llm_wq,
    llm_wk,
    llm_wv,
    llm_bq,
    llm_bk,
    llm_bv,
):
    n_tm = lax.axis_size("tm")
    n_t = lax.axis_size("tensor")
    me = lax.axis_index("tm")
    count = FRAMES // POOL
    owners = lax.dynamic_slice_in_dim(owner_map, me * count, count, 0)[:, 0]
    owners = jnp.pad(owners, (0, POOLED - count), constant_values=-n_tm)[None, :]
    return run_block(
        n_tm,
        n_t,
        enc_frames,
        enc_wq,
        enc_wk,
        enc_wv,
        adapter,
        enc_wo,
        text_embeds,
        jnp.asarray(rope_table()),
        enc_gain,
        owners,
        span_counts,
        llm_gain,
        llm_wq,
        llm_wk,
        llm_wv,
        llm_bq,
        llm_bk,
        llm_bv,
    )


def solution(mesh):
    placed = (
        P("tm", None),
        P(),
        P(),
        P(None, "tensor"),
        P(None, "tensor"),
        P(None, "tensor"),
        P("tensor", None),
        P(None, "tensor"),
        P(),
        P("tm", None),
        P(),
        P("tm", "tensor"),
        P("tm", "tensor"),
        P("tm", "tensor"),
        P("tensor"),
        P("tensor"),
        P("tensor"),
    )
    return jax.shard_map(
        shards, mesh=mesh, in_specs=placed, out_specs=P("tm", "tensor"), check_vma=False
    )
```
